1024 devices in a mesh: grp: 32 (over z, core), node: 32 (over y, x).
Axes of the slice: x: 4, y: 8, z: 16, core: 2. Of those that a mesh axis runs over, the one named last changes fastest.
Arguments:
- out_grad: bfloat16 [2048, 7168], P(('grp', 'node')), may hold values from -6 to 6
- expert_ids: int32 [2048, 8], P(('grp', 'node')), may hold values from 0 to 31, as said below
- slot_ids: int32 [2048, 8], P(('grp', 'node')), may hold values from -1 to 511, as said below
- gate_q: int32 [2048, 8], P(('grp', 'node')), may hold values from 1 to 255
- saved_x: bfloat16 [32, 512, 7168], P('grp'), may hold values from -6 to 6
- w_gate: bfloat16 [32, 7168, 2048], P('grp', None, 'node'), may hold values from -0.0625 to 0.0625
- w_up: bfloat16 [32, 7168, 2048], P('grp', None, 'node'), may hold values from -0.0625 to 0.0625
- w_down: bfloat16 [32, 2048, 7168], P('grp', 'node'), may hold values from -0.125 to 0.125
Outputs:
- in_grad: bfloat16 [2048, 7168], P(('grp', 'node'))
The draws below stay inside these ranges and needn't reach their ends.
Inputs may be any that keep to these rules, and one draw needn't show every extreme that they name: `expert_ids`: each token names 8 different experts, all within at most 4 groups of 4 consecutive experts. `slot_ids`: -1 marks a dropped choice. Kept choices of one expert hold different slots, and a token held by a device at node index n has its slots in n * 16 to (n + 1) * 16 - 1. In every draw some expert has all 16 slots of every node index filled.
All inputs are finite; a program needn't handle non-finite values.
Results may differ from the reference program's by a relative error of at most 0.023.
Values may be sent and summed in bfloat16 or wider, within the bound.
No kernel may reach another device: no remote copies, remote signals or barrier semaphores. Data moves between devices by JAX's collectives and lax.ppermute only.
A program may use at most 128 MiB of HBM per device.

```python
import jax
import jax.numpy as jnp
from jax import lax

D = 7168
FF = 2048
TOPK = 8
GROUP_EXP = 4
TOK_DEV = 2
EXPERTS = 32
GROUPS = 8
TOPG = 4
F_DEV = 64
CAPN = 16
CAP = 512
TOKENS = 2048
N_GRP = 32
N_NODE = 32


def routing(key):
    key_hot, key_gbias, key_gscore, key_ebias, key_escore, key_order = jax.random.split(key, 6)
    token_index = jnp.arange(TOKENS, dtype=jnp.int32)
    device_index = token_index // TOK_DEV
    token_row = device_index // N_NODE
    token_col = device_index % N_NODE
    column_pos = token_row * TOK_DEV + token_index % TOK_DEV
    forced = column_pos <= CAPN
    hot_expert = jax.random.randint(key_hot, (), 0, EXPERTS)
    group_index = jnp.arange(GROUPS, dtype=jnp.int32)
    group_bias = jax.random.randint(key_gbias, (GROUPS,), 0, 1024)
    group_score = jax.random.randint(key_gscore, (TOKENS, GROUPS), 0, 1024) + group_bias[None, :]
    group_score = group_score + jnp.where(forced[:, None] & (group_index[None, :] == hot_expert // GROUP_EXP), 1 << 22, 0)
    group_score = group_score * GROUPS + group_index[None, :]
    _, group_pick = lax.top_k(group_score, TOPG)
    group_list = jnp.sort(group_pick, axis=1).astype(jnp.int32)
    candidates = (group_list[:, :, None] * GROUP_EXP + jnp.arange(GROUP_EXP, dtype=jnp.int32)[None, None, :]).reshape(TOKENS, TOPG * GROUP_EXP)
    expert_bias = jax.random.randint(key_ebias, (EXPERTS,), 0, 2048)
    expert_score = jax.random.randint(key_escore, (TOKENS, TOPG * GROUP_EXP), 0, 1024) + expert_bias[candidates]
    expert_score = expert_score + jnp.where(forced[:, None] & (candidates == hot_expert), 1 << 22, 0)
    expert_score = expert_score * EXPERTS + candidates
    _, expert_pick = lax.top_k(expert_score, TOPK)
    expert_ids = jnp.take_along_axis(candidates, expert_pick, axis=1).astype(jnp.int32)
    priority = jax.random.permutation(key_order, TOKENS).astype(jnp.int32)
    ordering = jnp.argsort(token_col * TOKENS + priority)
    picks = jnp.any(expert_ids[:, :, None] == jnp.arange(EXPERTS, dtype=jnp.int32)[None, None, :], axis=1).astype(jnp.int32)
    column_size = N_GRP * TOK_DEV
    sorted_picks = picks[ordering].reshape(N_NODE, column_size, EXPERTS)
    before_count = jnp.cumsum(sorted_picks, axis=1) - sorted_picks
    inverse = jnp.argsort(ordering)
    ranking = before_count.reshape(TOKENS, EXPERTS)[inverse]
    pair_rank = jnp.take_along_axis(ranking, expert_ids, axis=1)
    slot_ids = jnp.where(pair_rank < CAPN, token_col[:, None] * CAPN + pair_rank, -1).astype(jnp.int32)
    return (expert_ids, slot_ids)


def draw_expert_ids(key, part):
    routed = routing(key)
    return routed[0]


def draw_slot_ids(key, part):
    routed = routing(key)
    return routed[1]


def set_ends(drawn, own_key, smallest, high):
    place = [jax.random.randint(jax.random.fold_in(own_key, axis), (), 0, length) for axis, length in enumerate(drawn.shape)]
    longest = drawn.shape.index(max(drawn.shape))
    neighbour = place[:longest] + [(place[longest] + 1) % drawn.shape[longest]] + place[longest + 1:]
    return drawn.at[tuple(place)].set(smallest).at[tuple(neighbour)].set(high)


def steps_of(own_key, dims, cuts, low, top_value):
    level = 1.0
    for position, blocks in cuts:
        heights = jax.random.uniform(jax.random.fold_in(jax.random.fold_in(own_key, 6), position), (blocks,), jnp.float32, low / len(cuts), top_value / len(cuts))
        level = level * jnp.repeat(jnp.exp(heights), dims[position] // blocks).reshape((-1,) + (1,) * (len(dims) - 1 - position))
    return level


def normal_values(rng, dims, width, reach, cuts=(), kind=jnp.bfloat16):
    result = jax.random.normal(rng, dims, jnp.float32) * width
    if len(cuts) > 0:
        result = steps_of(rng, dims, cuts, -0.22, 0.18) * result
    return jnp.clip(result, min=-reach, max=reach).astype(kind)


def setup_inputs(seed: int = 0) -> dict:
    splits = jax.random.split(jax.random.key(seed), 9)
    return {
        "out_grad": normal_values(splits[0], (TOKENS, D), 1.0, 6.0, ((0, 1024),)),
        "expert_ids": draw_expert_ids(jax.random.fold_in(splits[8], 71), 0),
        "slot_ids": draw_slot_ids(jax.random.fold_in(splits[8], 71), 0),
        "gate_q": set_ends(jax.random.randint(splits[3], (TOKENS, TOPK), 1, 256), jax.random.fold_in(splits[3], 1), 1, 255).astype(jnp.int32),
        "saved_x": normal_values(splits[4], (EXPERTS, CAP, D), 1.0, 6.0, ((0, 32),)),
        "w_gate": normal_values(splits[5], (EXPERTS, D, FF), D ** -0.5, 0.0625, ((0, 32), (2, 32))),
        "w_up": normal_values(splits[6], (EXPERTS, D, FF), D ** -0.5, 0.0625, ((0, 32), (2, 32))),
        "w_down": normal_values(splits[7], (EXPERTS, FF, D), FF ** -0.5, 0.125, ((0, 32), (1, 32))),
    }


def one_expert(operands):
    slot_rows, slot_gate, input_rows, gate_proj, up_proj, down_proj = operands
    pre_gate = jnp.dot(input_rows, gate_proj, preferred_element_type=jnp.float32)
    pre_up = jnp.dot(input_rows, up_proj, preferred_element_type=jnp.float32)
    grad_hidden = jnp.dot(slot_rows, down_proj.T, preferred_element_type=jnp.float32) * slot_gate[:, None]
    squash = jax.nn.sigmoid(pre_gate)
    grad_gate = (grad_hidden * pre_up * squash * (1.0 + pre_gate * (1.0 - squash))).astype(jnp.bfloat16)
    grad_up = (grad_hidden * pre_gate * squash).astype(jnp.bfloat16)
    gate_blocks = grad_gate.astype(jnp.float32).reshape(CAP, N_NODE, F_DEV)
    up_blocks = grad_up.astype(jnp.float32).reshape(CAP, N_NODE, F_DEV)
    gate_weights = gate_proj.astype(jnp.float32).reshape(D, N_NODE, F_DEV)
    up_weights = up_proj.astype(jnp.float32).reshape(D, N_NODE, F_DEV)
    shard_terms = jnp.einsum("pjf,djf->jpd", gate_blocks, gate_weights, precision=lax.Precision.HIGHEST)
    shard_terms = shard_terms + jnp.einsum("pjf,djf->jpd", up_blocks, up_weights, precision=lax.Precision.HIGHEST)
    rounded = lax.optimization_barrier(shard_terms.astype(jnp.bfloat16))
    return jnp.sum(rounded.astype(jnp.float32), axis=0).astype(jnp.bfloat16)


def reference(out_grad, expert_ids, slot_ids, gate_q, saved_x, w_gate, w_up, w_down):
    usable = slot_ids >= 0
    safe_slot = jnp.where(usable, slot_ids, CAP).astype(jnp.int32)
    gate_scale = gate_q.astype(jnp.float32) / 256.0
    spread = jnp.broadcast_to(out_grad[:, None, :], (TOKENS, TOPK, D))
    grad_rows = jnp.zeros((EXPERTS, CAP, D), jnp.bfloat16).at[expert_ids, safe_slot].set(spread, mode="drop")
    slot_gate = jnp.zeros((EXPERTS, CAP), jnp.float32).at[expert_ids, safe_slot].set(gate_scale, mode="drop")
    slot_dx = lax.map(one_expert, (grad_rows, slot_gate, saved_x, w_gate, w_up, w_down))
    picked = slot_dx[expert_ids, jnp.clip(safe_slot, 0, CAP - 1)]
    picked = jnp.where(usable[:, :, None], picked.astype(jnp.float32), jnp.float32(0.0))
    return jnp.sum(picked, axis=1).astype(jnp.bfloat16)
```

```python
import jax
import jax.numpy as jnp
from jax import lax
from jax.sharding import PartitionSpec as P

X_DEV = 4
C_DEV = 2
META = 128


def groups(axis_size, inner):
    outer = axis_size // inner
    along_outer = [[o * inner + i for o in range(outer)] for i in range(inner)]
    along_inner = [[o * inner + i for i in range(inner)] for o in range(outer)]
    return along_outer, along_inner


def swap(a, axis, members):
    return lax.all_to_all(a, axis, 0, 0, axis_index_groups=members, tiled=True)


def local(out_grad, expert_ids, slot_ids, gate_q, saved_x, w_gate, w_up, w_down):
    f32, bf16 = jnp.float32, jnp.bfloat16
    n_grp, n_node = lax.axis_size("grp"), lax.axis_size("node")
    my_expert, my_node = lax.axis_index("grp"), lax.axis_index("node")
    n_y, n_z = n_node // X_DEV, n_grp // C_DEV
    along_y, along_x = groups(n_node, X_DEV)
    along_z, along_c = groups(n_grp, C_DEV)
    n_tok, width = out_grad.shape
    part = width // n_y
    n_slot = saved_x.shape[1]
    per_node = n_slot // n_node
    n_hid = w_down.shape[1]
    n_pick = expert_ids.shape[1]

    down = w_down[0].reshape(n_hid, n_y, part).transpose(1, 0, 2)
    both_cut = jnp.concatenate(
        [
            w[0].T.reshape(n_hid, n_y, part).transpose(1, 0, 2)
            for w in (w_gate, w_up)
        ],
        axis=1,
    )
    down_y = swap(down, "node", along_y).reshape(n_y * n_hid, part)
    both_y = swap(both_cut, "node", along_y).reshape(n_y * 2 * n_hid, part)

    slot_here = jnp.where(slot_ids >= 0, slot_ids - my_node * per_node, -1)
    meta = jnp.concatenate([expert_ids, slot_here, gate_q], axis=1).astype(bf16)
    meta = jnp.pad(meta, ((0, 0), (0, META - 3 * n_pick)))
    cut = out_grad.reshape(n_tok, n_y, part).transpose(1, 0, 2)
    payload = jnp.concatenate(
        [cut, jnp.broadcast_to(meta[None], (n_y, n_tok, META))], axis=2
    )
    payload = swap(payload, "node", along_y).reshape(n_y * n_tok, part + META)
    tokens = lax.all_gather(payload, "grp", axis=0, tiled=True)
    n_all = n_grp * n_y * n_tok
    rout = tokens[:, part:].astype(f32)
    hit = rout[:, :n_pick] == my_expert.astype(f32)
    slot_of = rout[:, n_pick : 2 * n_pick]
    hit = hit & (slot_of >= 0)
    place = jnp.sum(jnp.where(hit, slot_of + 1, 0), axis=1).astype(jnp.int32) - 1
    gate = jnp.sum(jnp.where(hit, rout[:, 2 * n_pick : 3 * n_pick], 0), axis=1) / 256.0
    from_y = (jnp.arange(n_all, dtype=jnp.int32) // n_tok) % n_y
    place = jnp.where(place >= 0, place + from_y * per_node, -1)
    n_own = n_y * per_node
    one_hot = place[:, None] == jnp.arange(n_own, dtype=jnp.int32)[None, :]
    back_hot = jnp.where(one_hot, gate[:, None], 0.0).astype(bf16)
    back_hot = back_hot.reshape(n_z, C_DEV, n_y * n_tok, n_own).transpose(1, 0, 2, 3)
    back_hot = back_hot.reshape(n_all, n_own)
    rows = lax.dot_general(
        one_hot.astype(bf16),
        tokens[:, :part],
        (((0,), (0,)), ((), ())),
        preferred_element_type=f32,
    ).astype(bf16)

    all_rows = lax.all_gather(rows, "node", axis=0, axis_index_groups=along_x, tiled=True)
    last = (((1,), (1,)), ((), ()))
    hidden = lax.dot_general(down_y, all_rows, last, preferred_element_type=f32)
    hidden = swap(hidden.astype(bf16), "node", along_y)
    hidden = jnp.sum(hidden.reshape(n_y, n_hid, n_slot).astype(f32), axis=0)

    def forward(w):
        pre = jnp.dot(saved_x[0], w[0], preferred_element_type=f32)
        pre = pre.reshape(n_y, X_DEV, per_node, n_hid).transpose(1, 0, 2, 3)
        return pre.reshape(n_slot, n_hid).T

    pre_gate, pre_up = forward(w_gate), forward(w_up)
    squash = jax.nn.sigmoid(pre_gate)
    grad_gate = hidden * pre_up * squash * (1.0 + pre_gate * (1.0 - squash))
    grad_up = hidden * pre_gate * squash
    grads = jnp.concatenate([grad_gate, grad_up], axis=0).astype(bf16)
    all_grads = lax.all_gather(grads, "node", axis=0, axis_index_groups=along_y, tiled=True)

    slot_dx = lax.dot_general(
        all_grads, both_y, (((0,), (0,)), ((), ())), preferred_element_type=f32
    ).astype(bf16)
    slot_dx = swap(slot_dx, "node", along_x).reshape(X_DEV, n_own, part)
    slot_dx = jnp.sum(slot_dx.astype(f32), axis=0).astype(bf16)

    back = jnp.dot(back_hot, slot_dx, preferred_element_type=f32).astype(bf16)
    back = swap(back, "grp", along_c).reshape(C_DEV, n_all // C_DEV, part)
    back = jnp.sum(back.astype(f32), axis=0).astype(bf16)
    back = swap(back, "grp", along_z).reshape(n_z, n_y * n_tok, part)
    back = jnp.sum(back.astype(f32), axis=0).astype(bf16)
    back = swap(back.reshape(n_y, n_tok, part), "node", along_y)
    return back.transpose(1, 0, 2).reshape(n_tok, width)


def solution(mesh):
    in_specs = (
        P(("grp", "node"), None),
        P(("grp", "node"), None),
        P(("grp", "node"), None),
        P(("grp", "node"), None),
        P("grp", None, None),
        P("grp", None, "node"),
        P("grp", None, "node"),
        P("grp", "node", None),
    )
    out_specs = P(("grp", "node"), None)
    return jax.shard_map(local, mesh=mesh, in_specs=in_specs, out_specs=out_specs, check_vma=False)
```

```python
import functools

import jax
import jax.numpy as jnp
from jax import lax
from jax.experimental import pallas as pl
from jax.experimental.pallas import tpu as pltpu
from jax.sharding import PartitionSpec as P

SPLIT = 8
C_DEV = 2
Z_NEAR = 4
META = 128
VMEM = 48 * 1024 * 1024
f32, bf16 = jnp.float32, jnp.bfloat16


def call(body, out_shape, cost, **kw):
    flops, moved = cost
    return pl.pallas_call(
        body,
        out_shape=out_shape,
        compiler_params=pltpu.CompilerParams(vmem_limit_bytes=VMEM),
        cost_estimate=pl.CostEstimate(
            flops=flops, bytes_accessed=moved, transcendentals=0
        ),
        **kw,
    )


def swap(a, axis, members):
    return lax.all_to_all(a, axis, 0, 0, axis_index_groups=members, tiled=True)


def rounds(blocks, axis, moves):
    return [blocks[0]] + [
        lax.ppermute(block, axis, move) for block, move in zip(blocks[1:], moves)
    ]


def total(blocks):
    return functools.reduce(lambda p, q: p + q, [b.astype(f32) for b in blocks]).astype(bf16)


def cut_body(gate_ref, up_ref, down_ref, out_ref):
    n = gate_ref.shape[0]
    out_ref[0, :n] = gate_ref[...]
    out_ref[0, n : 2 * n] = up_ref[...]
    out_ref[0, 2 * n :] = down_ref[...]


def cut_weights(gate, up, down):
    n_hid, width = gate.shape
    part = width // SPLIT
    spec = pl.BlockSpec((n_hid, part), lambda i: (0, i))
    return call(
        cut_body,
        jax.ShapeDtypeStruct((SPLIT, 3 * n_hid, part), bf16),
        (0, 12 * n_hid * width),
        grid=(SPLIT,),
        in_specs=[spec] * 3,
        out_specs=pl.BlockSpec((1, 3 * n_hid, part), lambda i: (i, 0, 0)),
    )(gate, up, down)


def forward_body(x_ref, gate_ref, up_ref, out_ref, acc):
    step = pl.program_id(0)
    n = gate_ref.shape[0]
    both = jnp.concatenate([gate_ref[...], up_ref[...]], axis=0)
    term = lax.dot_general(
        both, x_ref[...], (((1,), (1,)), ((), ())), preferred_element_type=f32
    )

    @pl.when(step == 0)
    def _():
        acc[...] = term

    @pl.when(step > 0)
    def _():
        acc[...] += term

    @pl.when(step == pl.num_programs(0) - 1)
    def _():
        pre_gate, pre_up = acc[:n], acc[n:]
        squash = jax.nn.sigmoid(pre_gate)
        out_ref[:n] = pre_up * squash * (1.0 + pre_gate * (1.0 - squash))
        out_ref[n:] = pre_gate * squash


def forward(x, gate, up):
    n_slot, width = x.shape
    n_hid = gate.shape[0]
    part = width // 8
    spec = pl.BlockSpec((n_hid, part), lambda i: (0, i))
    return call(
        forward_body,
        jax.ShapeDtypeStruct((2 * n_hid, n_slot), f32),
        (4 * n_hid * n_slot * width, 2 * (n_slot + 2 * n_hid) * width),
        grid=(8,),
        in_specs=[pl.BlockSpec((n_slot, part), lambda i: (0, i)), spec, spec],
        out_specs=pl.BlockSpec((2 * n_hid, n_slot), lambda i: (0, 0)),
        scratch_shapes=[pltpu.VMEM((2 * n_hid, n_slot), f32)],
    )(x, gate, up)


def select_body(n_tok, per_node, n_pick, expert_ref, here_ref, there_ref, rows_ref, hot_ref):
    part = rows_ref.shape[1]
    tok = jnp.concatenate([here_ref[...], there_ref[...]], axis=0)
    rout = tok[:, part:].astype(f32)
    lane = lax.broadcasted_iota(jnp.int32, rout.shape, 1)
    row = lax.broadcasted_iota(jnp.int32, rout.shape, 0)
    slot = pltpu.roll(rout, META - n_pick, 1)
    gate = pltpu.roll(rout, META - 2 * n_pick, 1)
    hit = (lane < n_pick) & (rout == expert_ref[0].astype(f32)) & (slot >= 0)
    found = jnp.sum(jnp.where(hit, slot + 1.0, 0.0), axis=1, keepdims=True)
    scale = jnp.sum(jnp.where(hit, gate, 0.0), axis=1, keepdims=True) * (1.0 / 256.0)
    found = found.astype(jnp.int32) - 1
    node = (row // n_tok) % SPLIT
    one_hot = (found >= 0) & (node * per_node + found == lane)
    hot_ref[...] = jnp.where(one_hot, scale, 0.0).astype(bf16)
    pick = jnp.where(one_hot, 1.0, 0.0).T.astype(bf16)
    rows_ref[...] = jnp.dot(pick, tok[:, :part], preferred_element_type=f32).astype(bf16)


def select(expert, here, there, n_tok, per_node, n_pick):
    n_all, wide = 2 * here.shape[0], here.shape[1]
    part = wide - META
    n_own = SPLIT * per_node
    return call(
        functools.partial(select_body, n_tok, per_node, n_pick),
        (
            jax.ShapeDtypeStruct((n_own, part), bf16),
            jax.ShapeDtypeStruct((n_all, n_own), bf16),
        ),
        (2 * n_all * n_own * part, 2 * n_all * wide),
        in_specs=[
            pl.BlockSpec(memory_space=pltpu.SMEM),
            pl.BlockSpec(memory_space=pltpu.VMEM),
            pl.BlockSpec(memory_space=pltpu.VMEM),
        ],
        out_specs=[pl.BlockSpec(memory_space=pltpu.VMEM)] * 2,
    )(expert, here, there)


def hidden_body(w_ref, rows_ref, out_ref):
    n, h, part = w_ref.shape
    got = lax.dot_general(
        w_ref[...].reshape(n * h, part),
        rows_ref[...],
        (((1,), (1,)), ((), ())),
        preferred_element_type=f32,
    )
    out_ref[...] = got.astype(bf16)


def hidden_part(weights, rows):
    n, h3, part = weights.shape
    h = h3 // 3
    n_slot = rows.shape[0]
    half = n_slot // 2
    return call(
        hidden_body,
        jax.ShapeDtypeStruct((n * h, n_slot), bf16),
        (2 * n * h * n_slot * part, 2 * (n * h + n_slot) * part),
        grid=(2,),
        in_specs=[
            pl.BlockSpec((n, h, part), lambda i: (0, 2, 0)),
            pl.BlockSpec((half, part), lambda i: (i, 0)),
        ],
        out_specs=pl.BlockSpec((n * h, half), lambda i: (0, i)),
    )(weights, rows)


def grads_body(parts_ref, coef_ref, out_ref):
    n, h, _ = parts_ref.shape
    total = jnp.sum(parts_ref[...].astype(f32), axis=0)
    grads = jnp.concatenate([total * coef_ref[:h], total * coef_ref[h:]], axis=0)
    grads = grads.T.astype(bf16)
    for i in range(n):
        out_ref[i] = grads


def grads_of(parts, coef):
    n, h, n_slot = parts.shape
    return call(
        grads_body,
        jax.ShapeDtypeStruct((n, n_slot, 2 * h), bf16),
        (2 * n * h * n_slot, 6 * n * h * n_slot),
    )(parts, coef)


def slot_body(grads_ref, w_ref, out_ref):
    n, h, part = w_ref.shape
    grads = jnp.concatenate([grads_ref[i] for i in range(n)], axis=1)
    got = jnp.dot(grads, w_ref[...].reshape(n * h, part), preferred_element_type=f32)
    out_ref[...] = got.astype(bf16)


def slot_part(grads, weights):
    n, n_slot, h2 = grads.shape
    part = weights.shape[2]
    half = n_slot // 2
    return call(
        slot_body,
        jax.ShapeDtypeStruct((n_slot, part), bf16),
        (2 * n * h2 * n_slot * part, 2 * (n * h2 * (n_slot + part) + n_slot * part)),
        grid=(2,),
        in_specs=[
            pl.BlockSpec((n, half, h2), lambda i: (0, i, 0)),
            pl.BlockSpec((n, h2, part), lambda i: (0, 0, 0)),
        ],
        out_specs=pl.BlockSpec((half, part), lambda i: (i, 0)),
    )(grads, weights)


def back_body(hot_ref, parts_ref, here_ref, there_ref):
    own = jnp.sum(parts_ref[...].astype(f32), axis=0).astype(bf16)
    got = jnp.dot(hot_ref[...], own, preferred_element_type=f32).astype(bf16)
    half = here_ref.shape[0]
    here_ref[...] = got[:half]
    there_ref[...] = got[half:]


def back_rows(hot, parts):
    n_all, n_own = hot.shape
    part = parts.shape[2]
    return call(
        back_body,
        (jax.ShapeDtypeStruct((n_all // 2, part), bf16),) * 2,
        (2 * n_all * n_own * part, 2 * (n_all * part + parts.size)),
    )(hot, parts)


def local(out_grad, expert_ids, slot_ids, gate_q, saved_x, w_gate, w_up, w_down):
    n_grp, n_node = lax.axis_size("grp"), lax.axis_size("node")
    my_expert, my_node = lax.axis_index("grp"), lax.axis_index("node")
    n_rest, n_z = n_node // SPLIT, n_grp // C_DEV
    z_far = n_z // Z_NEAR
    block = [[h * SPLIT + d for d in range(SPLIT)] for h in range(n_rest)]
    rest = [[h * SPLIT + d for h in range(n_rest)] for d in range(SPLIT)]
    at = lambda far, near, c: (far * Z_NEAR + near) * C_DEV + c
    devices = [(f, n, c) for f in range(z_far) for n in range(Z_NEAR) for c in range(C_DEV)]
    far = [[(at(f, n, c), at((f + k) % z_far, n, c)) for f, n, c in devices] for k in range(1, z_far)]
    near = [[(at(f, n, c), at(f, (n + j) % Z_NEAR, c)) for f, n, c in devices] for j in range(1, Z_NEAR)]
    other = [(at(f, n, c), at(f, n, C_DEV - 1 - c)) for f, n, c in devices]
    undo = lambda moves: [[(to, frm) for frm, to in move] for move in moves]
    n_tok, width = out_grad.shape
    part = width // SPLIT
    n_slot = saved_x.shape[1]
    per_node = n_slot // n_node
    n_hid = w_down.shape[1]
    n_pick = expert_ids.shape[1]
    n_own = SPLIT * per_node
    gate, up, down = w_gate[0].T, w_up[0].T, w_down[0]

    slot_here = jnp.where(slot_ids >= 0, slot_ids - my_node * per_node, -1)
    meta = jnp.concatenate([expert_ids, slot_here, gate_q], axis=1).astype(bf16)
    meta = jnp.pad(meta, ((0, 0), (0, META - 3 * n_pick)))
    cols = out_grad.reshape(n_tok, SPLIT, part).transpose(1, 0, 2)
    payload = jnp.concatenate(
        [cols, jnp.broadcast_to(meta[None], (SPLIT, n_tok, META))], axis=2
    )
    payload = swap(payload, "node", block).reshape(SPLIT * n_tok, part + META)

    weights = cut_weights(gate, up, down)
    payload, weights = lax.optimization_barrier((payload, weights))
    weights = swap(weights, "node", block)

    tokens = jnp.concatenate(rounds([payload] * z_far, "grp", far), axis=0)
    tokens = jnp.concatenate(rounds([tokens] * Z_NEAR, "grp", near), axis=0)
    there = lax.ppermute(tokens, "grp", other)
    expert = my_expert.astype(jnp.int32).reshape(1)
    rows, hot = select(expert, tokens, there, n_tok, per_node, n_pick)
    rows = lax.all_gather(rows, "node", axis=0, axis_index_groups=rest, tiled=True)

    hidden = hidden_part(weights, rows)
    hidden = swap(hidden, "node", block).reshape(SPLIT, n_hid, n_slot)
    coef = forward(saved_x[0], gate, up)
    grads = swap(grads_of(hidden, coef), "node", block)
    parts = swap(slot_part(grads, weights), "node", rest)

    here, there = back_rows(hot, parts.reshape(n_rest, n_own, part))
    back = total([here, lax.ppermute(there, "grp", other)])
    back = total(rounds(jnp.split(back, Z_NEAR), "grp", undo(near)))
    back = total(rounds(jnp.split(back, z_far), "grp", undo(far)))
    back = swap(back.reshape(SPLIT, n_tok, part), "node", block)
    return back.transpose(1, 0, 2).reshape(n_tok, width)


def solution(mesh):
    in_specs = (
        P(("grp", "node"), None),
        P(("grp", "node"), None),
        P(("grp", "node"), None),
        P(("grp", "node"), None),
        P("grp", None, None),
        P("grp", None, "node"),
        P("grp", None, "node"),
        P("grp", "node", None),
    )
    out_specs = P(("grp", "node"), None)
    return jax.shard_map(local, mesh=mesh, in_specs=in_specs, out_specs=out_specs, check_vma=False)
```

```python
import functools

import jax
import jax.numpy as jnp
from jax import lax
from jax.experimental import pallas as pl
from jax.experimental.pallas import tpu as pltpu
from jax.sharding import PartitionSpec as P

SPLIT = 8
C_DEV = 2
META = 128
VMEM = 48 * 1024 * 1024
f32, bf16 = jnp.float32, jnp.bfloat16


def call(body, out_shape, cost, **kw):
    flops, moved = cost
    return pl.pallas_call(
        body,
        out_shape=out_shape,
        compiler_params=pltpu.CompilerParams(vmem_limit_bytes=VMEM),
        cost_estimate=pl.CostEstimate(
            flops=flops, bytes_accessed=moved, transcendentals=0
        ),
        **kw,
    )


def hbm(*arrays):
    return [pltpu.with_memory_space_constraint(a, pltpu.HBM) for a in arrays]


def swap(a, axis, members):
    return lax.all_to_all(a, axis, 0, 0, axis_index_groups=members, tiled=True)


def total(blocks):
    return functools.reduce(lambda p, q: p + q, [b.astype(f32) for b in blocks]).astype(bf16)


def pack_body(per_node, node_ref, grad_ref, ids_ref, slots_ref, gates_ref, out_ref, held):
    n_tok, n_pick = ids_ref.shape
    part = out_ref.shape[1] - META
    slots = slots_ref[...]
    slots = jnp.where(slots >= 0, slots - node_ref[0] * per_node, -1)
    held[...] = jnp.zeros_like(held)
    grad = grad_ref[...].astype(f32)
    for i in range(SPLIT):
        rows = slice(i * n_tok, (i + 1) * n_tok)
        held[rows, :part] = grad[:, i * part : (i + 1) * part]
        for j, field in enumerate((ids_ref[...], slots, gates_ref[...])):
            held[rows, part + j * n_pick : part + (j + 1) * n_pick] = field.astype(f32)
    out_ref[...] = held[...].astype(bf16)


def pack(node, grad, ids, slots, gates, per_node):
    n_tok, width = grad.shape
    shape = (SPLIT * n_tok, width // SPLIT + META)
    return call(
        functools.partial(pack_body, per_node),
        jax.ShapeDtypeStruct(shape, bf16),
        (0, 4 * n_tok * width),
        in_specs=[pl.BlockSpec(memory_space=pltpu.SMEM)]
        + [pl.BlockSpec(memory_space=pltpu.VMEM)] * 4,
        out_specs=pl.BlockSpec(memory_space=pltpu.VMEM),
        scratch_shapes=[pltpu.VMEM(shape, f32)],
    )(node, grad, ids, slots, gates)


def cut_body(gate_ref, up_ref, down_ref, out_ref):
    n = gate_ref.shape[0]
    out_ref[0, :n] = gate_ref[...]
    out_ref[0, n : 2 * n] = up_ref[...]
    out_ref[0, 2 * n :] = down_ref[...]


def cut_weights(gate, up, down):
    n_hid, width = gate.shape
    part = width // SPLIT
    spec = pl.BlockSpec((n_hid, part), lambda i: (0, i))
    return call(
        cut_body,
        pltpu.HBM((SPLIT, 3 * n_hid, part), bf16),
        (0, 12 * n_hid * width),
        grid=(SPLIT,),
        in_specs=[spec] * 3,
        out_specs=pl.BlockSpec((1, 3 * n_hid, part), lambda i: (i, 0, 0)),
    )(*hbm(gate, up, down))


def forward_body(x_ref, gate_ref, up_ref, out_ref, acc):
    step = pl.program_id(0)
    n = gate_ref.shape[0]
    both = jnp.concatenate([gate_ref[...], up_ref[...]], axis=0)
    term = lax.dot_general(
        both, x_ref[...], (((1,), (1,)), ((), ())), preferred_element_type=f32
    )

    @pl.when(step == 0)
    def _():
        acc[...] = term

    @pl.when(step > 0)
    def _():
        acc[...] += term

    @pl.when(step == pl.num_programs(0) - 1)
    def _():
        pre_gate, pre_up = acc[:n], acc[n:]
        squash = jax.nn.sigmoid(pre_gate)
        out_ref[:n] = pre_up * squash * (1.0 + pre_gate * (1.0 - squash))
        out_ref[n:] = pre_gate * squash


def forward(x, gate, up):
    n_slot, width = x.shape
    n_hid = gate.shape[0]
    part = width // 8
    spec = pl.BlockSpec((n_hid, part), lambda i: (0, i))
    return call(
        forward_body,
        jax.ShapeDtypeStruct((2 * n_hid, n_slot), f32),
        (4 * n_hid * n_slot * width, 2 * (n_slot + 2 * n_hid) * width),
        grid=(8,),
        in_specs=[pl.BlockSpec((n_slot, part), lambda i: (0, i)), spec, spec],
        out_specs=pl.BlockSpec((2 * n_hid, n_slot), lambda i: (0, 0)),
        scratch_shapes=[pltpu.VMEM((2 * n_hid, n_slot), f32)],
    )(*hbm(x, gate, up))


def select_body(n_tok, per_node, n_pick, expert_ref, here_ref, there_ref, rows_ref, hot_ref):
    part = rows_ref.shape[1]
    tok = jnp.concatenate([here_ref[...], there_ref[...]], axis=0)
    rout = tok[:, part:].astype(f32)
    lane = lax.broadcasted_iota(jnp.int32, rout.shape, 1)
    row = lax.broadcasted_iota(jnp.int32, rout.shape, 0)
    slot = pltpu.roll(rout, META - n_pick, 1)
    gate = pltpu.roll(rout, META - 2 * n_pick, 1)
    hit = (lane < n_pick) & (rout == expert_ref[0].astype(f32)) & (slot >= 0)
    found = jnp.sum(jnp.where(hit, slot + 1.0, 0.0), axis=1, keepdims=True)
    scale = jnp.sum(jnp.where(hit, gate, 0.0), axis=1, keepdims=True) * (1.0 / 256.0)
    found = found.astype(jnp.int32) - 1
    node = (row // n_tok) % SPLIT
    one_hot = (found >= 0) & (node * per_node + found == lane)
    hot_ref[...] = jnp.where(one_hot, scale, 0.0).astype(bf16)
    pick = jnp.where(one_hot, 1.0, 0.0).T.astype(bf16)
    rows = jnp.dot(pick, tok[:, :part], preferred_element_type=f32).astype(bf16)
    for i in range(rows_ref.shape[0] // rows.shape[0]):
        rows_ref[i * rows.shape[0] : (i + 1) * rows.shape[0]] = rows


def select(expert, here, there, n_rest, n_tok, per_node, n_pick):
    n_all, wide = 2 * here.shape[0], here.shape[1]
    part = wide - META
    n_own = SPLIT * per_node
    return call(
        functools.partial(select_body, n_tok, per_node, n_pick),
        (
            pltpu.HBM((n_rest * n_own, part), bf16),
            pltpu.HBM((n_all, n_own), bf16),
        ),
        (2 * n_all * n_own * part, 2 * n_all * wide),
        in_specs=[
            pl.BlockSpec(memory_space=pltpu.SMEM),
            pl.BlockSpec(memory_space=pltpu.VMEM),
            pl.BlockSpec(memory_space=pltpu.VMEM),
        ],
        out_specs=[pl.BlockSpec(memory_space=pltpu.VMEM)] * 2,
    )(expert, here, there)


def hidden_body(w_ref, rows_ref, out_ref):
    n, h, part = w_ref.shape
    got = lax.dot_general(
        w_ref[...].reshape(n * h, part),
        rows_ref[...],
        (((1,), (1,)), ((), ())),
        preferred_element_type=f32,
    )
    out_ref[...] = got.astype(bf16)


def hidden_part(weights, rows):
    n, h3, part = weights.shape
    h = h3 // 3
    n_slot = rows.shape[0]
    half = n_slot // 2
    return call(
        hidden_body,
        pltpu.HBM((n * h, n_slot), bf16),
        (2 * n * h * n_slot * part, 2 * (n * h + n_slot) * part),
        grid=(2,),
        in_specs=[
            pl.BlockSpec((n, h, part), lambda i: (0, 2, 0)),
            pl.BlockSpec((half, part), lambda i: (i, 0)),
        ],
        out_specs=pl.BlockSpec((n * h, half), lambda i: (0, i)),
    )(weights, rows)


def grads_body(parts_ref, coef_ref, out_ref):
    n, h, _ = parts_ref.shape
    total = jnp.sum(parts_ref[...].astype(f32), axis=0)
    grads = jnp.concatenate([total * coef_ref[:h], total * coef_ref[h:]], axis=0)
    grads = grads.T.astype(bf16)
    for i in range(n):
        out_ref[i] = grads


def grads_of(parts, coef):
    n, h, n_slot = parts.shape
    return call(
        grads_body,
        jax.ShapeDtypeStruct((n, n_slot, 2 * h), bf16),
        (2 * n * h * n_slot, 6 * n * h * n_slot),
    )(parts, coef)


def slot_body(grads_ref, w_ref, out_ref):
    n, h, part = w_ref.shape
    grads = jnp.concatenate([grads_ref[i] for i in range(n)], axis=1)
    got = jnp.dot(grads, w_ref[...].reshape(n * h, part), preferred_element_type=f32)
    out_ref[...] = got.astype(bf16)


def slot_part(grads, weights):
    n, n_slot, h2 = grads.shape
    part = weights.shape[2]
    half = n_slot // 2
    return call(
        slot_body,
        jax.ShapeDtypeStruct((n_slot, part), bf16),
        (2 * n * h2 * n_slot * part, 2 * (n * h2 * (n_slot + part) + n_slot * part)),
        grid=(2,),
        in_specs=[
            pl.BlockSpec((n, half, h2), lambda i: (0, i, 0)),
            pl.BlockSpec((n, h2, part), lambda i: (0, 0, 0)),
        ],
        out_specs=pl.BlockSpec((half, part), lambda i: (i, 0)),
    )(grads, weights)


def back_body(hot_ref, parts_ref, here_ref, there_ref):
    own = jnp.sum(parts_ref[...].astype(f32), axis=0).astype(bf16)
    got = jnp.dot(hot_ref[...], own, preferred_element_type=f32).astype(bf16)
    half = here_ref.shape[0]
    here_ref[...] = got[:half]
    there_ref[...] = got[half:]


def back_rows(hot, parts):
    n_all, n_own = hot.shape
    part = parts.shape[2]
    return call(
        back_body,
        (jax.ShapeDtypeStruct((n_all // 2, part), bf16),) * 2,
        (2 * n_all * n_own * part, 2 * (n_all * part + parts.size)),
    )(hot, parts)


def unpack_body(parts_ref, out_ref):
    n_tok = out_ref.shape[0]
    added = jnp.sum(parts_ref[...].astype(f32), axis=0)
    pieces = [added[i * n_tok : (i + 1) * n_tok] for i in range(SPLIT)]
    out_ref[...] = jnp.concatenate(pieces, axis=1).astype(bf16)


def unpack(parts, n_tok):
    return call(
        unpack_body,
        jax.ShapeDtypeStruct((n_tok, SPLIT * parts.shape[2]), bf16),
        (parts.size, 2 * parts.size),
    )(parts)


def local(out_grad, expert_ids, slot_ids, gate_q, saved_x, w_gate, w_up, w_down):
    n_grp, n_node = lax.axis_size("grp"), lax.axis_size("node")
    my_expert, my_node = lax.axis_index("grp"), lax.axis_index("node")
    n_rest, n_z = n_node // SPLIT, n_grp // C_DEV
    block = [[h * SPLIT + d for d in range(SPLIT)] for h in range(n_rest)]
    along_z = [[z * C_DEV + c for z in range(n_z)] for c in range(C_DEV)]
    other = [(z * C_DEV + c, z * C_DEV + 1 - c) for z in range(n_z) for c in range(C_DEV)]
    n_tok, width = out_grad.shape
    part = width // SPLIT
    n_slot = saved_x.shape[1]
    per_node = n_slot // n_node
    n_hid = w_down.shape[1]
    n_pick = expert_ids.shape[1]
    n_own = SPLIT * per_node
    gate, up, down = w_gate[0].T, w_up[0].T, w_down[0]

    payload = pack(my_node.astype(jnp.int32).reshape(1), out_grad, expert_ids, slot_ids, gate_q, per_node)

    weights = cut_weights(gate, up, down)
    payload, weights = lax.optimization_barrier((payload, weights))
    weights = swap(weights, "node", block)

    here = lax.all_gather(payload, "grp", axis=0, axis_index_groups=along_z, tiled=True)
    there = lax.ppermute(here, "grp", other)
    expert = my_expert.astype(jnp.int32).reshape(1)
    rows, hot = select(expert, here, there, n_rest, n_tok, per_node, n_pick)
    rows, weights = lax.optimization_barrier((rows, weights))
    rows = lax.all_to_all(rows, "node", 0, 0, tiled=True)

    coef = forward(saved_x[0], gate, up)
    hidden, coef = lax.optimization_barrier((hidden_part(weights, rows), coef))
    hidden = swap(hidden, "node", block).reshape(SPLIT, n_hid, n_slot)
    grads = swap(grads_of(hidden, coef), "node", block)
    parts = lax.all_to_all(slot_part(grads, weights), "node", 0, 0, tiled=True)

    here, there = back_rows(hot, parts.reshape(n_rest, n_own, part))
    back = total([here, lax.ppermute(there, "grp", other)])
    back = swap(back, "grp", along_z).reshape(n_z, SPLIT * n_tok, part)
    return unpack(back, n_tok)


def solution(mesh):
    in_specs = (
        P(("grp", "node"), None),
        P(("grp", "node"), None),
        P(("grp", "node"), None),
        P(("grp", "node"), None),
        P("grp", None, None),
        P("grp", None, "node"),
        P("grp", None, "node"),
        P("grp", "node", None),
    )
    out_specs = P(("grp", "node"), None)
    return jax.shard_map(local, mesh=mesh, in_specs=in_specs, out_specs=out_specs, check_vma=False)
```

```python
import functools

import jax
import jax.numpy as jnp
from jax import lax
from jax.experimental import pallas as pl
from jax.experimental.pallas import tpu as pltpu
from jax.sharding import PartitionSpec as P

SPLIT = 8
C_DEV = 2
META = 128
VMEM = 48 * 1024 * 1024
f32, bf16 = jnp.float32, jnp.bfloat16


def call(body, out_shape, cost, **kw):
    flops, moved = cost
    return pl.pallas_call(
        body,
        out_shape=out_shape,
        compiler_params=pltpu.CompilerParams(vmem_limit_bytes=VMEM),
        cost_estimate=pl.CostEstimate(
            flops=flops, bytes_accessed=moved, transcendentals=0
        ),
        **kw,
    )


def hbm(*arrays):
    return [pltpu.with_memory_space_constraint(a, pltpu.HBM) for a in arrays]


def swap(a, axis, members):
    return lax.all_to_all(a, axis, 0, 0, axis_index_groups=members, tiled=True)


def total(blocks):
    return functools.reduce(lambda p, q: p + q, [b.astype(f32) for b in blocks]).astype(bf16)


def pack_body(per_node, node_ref, grad_ref, ids_ref, slots_ref, gates_ref, out_ref, held):
    n_tok, n_pick = ids_ref.shape
    part = out_ref.shape[1] - META
    slots = slots_ref[...]
    slots = jnp.where(slots >= 0, slots - node_ref[0] * per_node, -1)
    held[...] = jnp.zeros_like(held)
    grad = grad_ref[...].astype(f32)
    for i in range(SPLIT):
        rows = slice(i * n_tok, (i + 1) * n_tok)
        held[rows, :part] = grad[:, i * part : (i + 1) * part]
        for j, field in enumerate((ids_ref[...], slots, gates_ref[...])):
            held[rows, part + j * n_pick : part + (j + 1) * n_pick] = field.astype(f32)
    out_ref[...] = held[...].astype(bf16)


def pack(node, grad, ids, slots, gates, per_node):
    n_tok, width = grad.shape
    shape = (SPLIT * n_tok, width // SPLIT + META)
    return call(
        functools.partial(pack_body, per_node),
        jax.ShapeDtypeStruct(shape, bf16),
        (0, 4 * n_tok * width),
        in_specs=[pl.BlockSpec(memory_space=pltpu.SMEM)]
        + [pl.BlockSpec(memory_space=pltpu.VMEM)] * 4,
        out_specs=pl.BlockSpec(memory_space=pltpu.VMEM),
        scratch_shapes=[pltpu.VMEM(shape, f32)],
    )(node, grad, ids, slots, gates)


def cut_body(gate_ref, up_ref, down_ref, out_ref, held, sem_in, sem_out):
    n = gate_ref.shape[0]
    part = out_ref.shape[2]
    come = [
        [
            pltpu.make_async_copy(
                ref.at[:, pl.ds(i * part, part)],
                held.at[i, pl.ds(j * n, n)],
                sem_in.at[i, j],
            )
            for j, ref in enumerate((gate_ref, up_ref, down_ref))
        ]
        for i in range(SPLIT)
    ]
    leave = [
        pltpu.make_async_copy(held.at[i], out_ref.at[i], sem_out.at[i])
        for i in range(SPLIT)
    ]
    for copies in come:
        for copy in copies:
            copy.start()
    for i in range(SPLIT):
        for copy in come[i]:
            copy.wait()
        leave[i].start()
    for copy in leave:
        copy.wait()


def cut_weights(gate, up, down):
    n_hid, width = gate.shape
    shape = (SPLIT, 3 * n_hid, width // SPLIT)
    return call(
        cut_body,
        pltpu.HBM(shape, bf16),
        (0, 12 * n_hid * width),
        in_specs=[pl.BlockSpec(memory_space=pl.ANY)] * 3,
        out_specs=pl.BlockSpec(memory_space=pl.ANY),
        scratch_shapes=[
            pltpu.VMEM(shape, bf16),
            pltpu.SemaphoreType.DMA((SPLIT, 3)),
            pltpu.SemaphoreType.DMA((SPLIT,)),
        ],
    )(*hbm(gate, up, down))


def forward_body(x_ref, gate_ref, up_ref, out_ref):
    n = gate_ref.shape[0]
    both = jnp.concatenate([gate_ref[...], up_ref[...]], axis=0)
    pre = lax.dot_general(
        x_ref[...], both, (((1,), (1,)), ((), ())), preferred_element_type=f32
    ).T
    pre_gate, pre_up = pre[:n], pre[n:]
    squash = jax.nn.sigmoid(pre_gate)
    out_ref[:n] = pre_up * squash * (1.0 + pre_gate * (1.0 - squash))
    out_ref[n:] = pre_gate * squash


def forward(x, gate, up):
    n_slot, width = x.shape
    n_hid = gate.shape[0]
    half = n_slot // 2
    spec = pl.BlockSpec((n_hid, width), lambda i: (0, 0))
    return call(
        forward_body,
        jax.ShapeDtypeStruct((2 * n_hid, n_slot), f32),
        (4 * n_hid * n_slot * width, 2 * (n_slot + 2 * n_hid) * width),
        grid=(2,),
        in_specs=[pl.BlockSpec((half, width), lambda i: (i, 0)), spec, spec],
        out_specs=pl.BlockSpec((2 * n_hid, half), lambda i: (0, i)),
    )(*hbm(x, gate, up))


def select_body(n_tok, per_node, n_pick, expert_ref, tok_ref, *refs):
    rows_ref, hot_ref = refs[-2:]
    part = rows_ref.shape[1]
    rout = tok_ref[:, part:].astype(f32)
    lane = lax.broadcasted_iota(jnp.int32, rout.shape, 1)
    row = lax.broadcasted_iota(jnp.int32, rout.shape, 0)
    slot = pltpu.roll(rout, META - n_pick, 1)
    gate = pltpu.roll(rout, META - 2 * n_pick, 1)
    hit = (lane < n_pick) & (rout == expert_ref[0].astype(f32)) & (slot >= 0)
    found = jnp.sum(jnp.where(hit, slot + 1.0, 0.0), axis=1, keepdims=True)
    scale = jnp.sum(jnp.where(hit, gate, 0.0), axis=1, keepdims=True) * (1.0 / 256.0)
    found = found.astype(jnp.int32) - 1
    node = (row // n_tok) % SPLIT
    one_hot = (found >= 0) & (node * per_node + found == lane)
    hot_ref[...] = jnp.where(one_hot, scale, 0.0).astype(bf16)
    pick = jnp.where(one_hot, 1.0, 0.0).T.astype(bf16)
    rows = jnp.dot(pick, tok_ref[:, :part], preferred_element_type=f32).astype(bf16)
    if len(refs) == 3:
        rows = rows + refs[0][...]
    for i in range(rows_ref.shape[0] // rows.shape[0]):
        rows_ref[i * rows.shape[0] : (i + 1) * rows.shape[0]] = rows


def select(expert, tokens, before, copies, n_tok, per_node, n_pick):
    n_all, wide = tokens.shape
    part = wide - META
    n_own = SPLIT * per_node
    return call(
        functools.partial(select_body, n_tok, per_node, n_pick),
        (
            (pltpu.HBM if before else jax.ShapeDtypeStruct)((copies * n_own, part), bf16),
            pltpu.HBM((n_all, n_own), bf16),
        ),
        (2 * n_all * n_own * part, 2 * n_all * wide),
        in_specs=[pl.BlockSpec(memory_space=pltpu.SMEM)]
        + [pl.BlockSpec(memory_space=pltpu.VMEM)] * (1 + len(before)),
        out_specs=[pl.BlockSpec(memory_space=pltpu.VMEM)] * 2,
    )(expert, tokens, *before)


def hidden_body(w_ref, rows_ref, out_ref):
    n, h, part = w_ref.shape
    got = lax.dot_general(
        w_ref[...].reshape(n * h, part),
        rows_ref[...],
        (((1,), (1,)), ((), ())),
        preferred_element_type=f32,
    )
    out_ref[...] = got.astype(bf16)


def hidden_part(weights, rows):
    n, h3, part = weights.shape
    h = h3 // 3
    n_slot = rows.shape[0]
    half = n_slot // 2
    return call(
        hidden_body,
        pltpu.HBM((n * h, n_slot), bf16),
        (2 * n * h * n_slot * part, 2 * (n * h + n_slot) * part),
        grid=(2,),
        in_specs=[
            pl.BlockSpec((n, h, part), lambda i: (0, 2, 0)),
            pl.BlockSpec((half, part), lambda i: (i, 0)),
        ],
        out_specs=pl.BlockSpec((n * h, half), lambda i: (0, i)),
    )(weights, rows)


def grads_body(parts_ref, coef_ref, out_ref):
    n, h, _ = parts_ref.shape
    total = jnp.sum(parts_ref[...].astype(f32), axis=0)
    grads = jnp.concatenate([total * coef_ref[:h], total * coef_ref[h:]], axis=0)
    grads = grads.T.astype(bf16)
    for i in range(n):
        out_ref[i] = grads


def grads_of(parts, coef):
    n, h, n_slot = parts.shape
    return call(
        grads_body,
        jax.ShapeDtypeStruct((n, n_slot, 2 * h), bf16),
        (2 * n * h * n_slot, 6 * n * h * n_slot),
    )(parts, coef)


def slot_body(grads_ref, w_ref, out_ref):
    n, h, part = w_ref.shape
    grads = jnp.concatenate([grads_ref[i] for i in range(n)], axis=1)
    got = jnp.dot(grads, w_ref[...].reshape(n * h, part), preferred_element_type=f32)
    out_ref[...] = got.astype(bf16)


def slot_part(grads, weights):
    n, n_slot, h2 = grads.shape
    part = weights.shape[2]
    half = n_slot // 2
    return call(
        slot_body,
        jax.ShapeDtypeStruct((n_slot, part), bf16),
        (2 * n * h2 * n_slot * part, 2 * (n * h2 * (n_slot + part) + n_slot * part)),
        grid=(2,),
        in_specs=[
            pl.BlockSpec((n, half, h2), lambda i: (0, i, 0)),
            pl.BlockSpec((n, h2, part), lambda i: (0, 0, 0)),
        ],
        out_specs=pl.BlockSpec((half, part), lambda i: (i, 0)),
    )(grads, weights)


def back_body(hot_here_ref, hot_there_ref, parts_ref, here_ref, there_ref):
    own = jnp.sum(parts_ref[...].astype(f32), axis=0).astype(bf16)
    for hot_ref, out_ref in ((hot_there_ref, there_ref), (hot_here_ref, here_ref)):
        got = jnp.dot(hot_ref[...], own, preferred_element_type=f32)
        out_ref[...] = got.astype(bf16)


def back_rows(hot_here, hot_there, parts):
    half, n_own = hot_here.shape
    part = parts.shape[2]
    return call(
        back_body,
        (jax.ShapeDtypeStruct((half, part), bf16),) * 2,
        (4 * half * n_own * part, 4 * half * part + 2 * parts.size),
    )(hot_here, hot_there, parts)


def unpack_body(parts_ref, out_ref):
    n_tok = out_ref.shape[0]
    added = jnp.sum(parts_ref[...].astype(f32), axis=0)
    pieces = [added[i * n_tok : (i + 1) * n_tok] for i in range(SPLIT)]
    out_ref[...] = jnp.concatenate(pieces, axis=1).astype(bf16)


def unpack(parts, n_tok):
    return call(
        unpack_body,
        jax.ShapeDtypeStruct((n_tok, SPLIT * parts.shape[2]), bf16),
        (parts.size, 2 * parts.size),
    )(parts)


def local(out_grad, expert_ids, slot_ids, gate_q, saved_x, w_gate, w_up, w_down):
    n_grp, n_node = lax.axis_size("grp"), lax.axis_size("node")
    my_expert, my_node = lax.axis_index("grp"), lax.axis_index("node")
    n_rest, n_z = n_node // SPLIT, n_grp // C_DEV
    block = [[h * SPLIT + d for d in range(SPLIT)] for h in range(n_rest)]
    along_z = [[z * C_DEV + c for z in range(n_z)] for c in range(C_DEV)]
    other = [(z * C_DEV + c, z * C_DEV + 1 - c) for z in range(n_z) for c in range(C_DEV)]
    n_tok, width = out_grad.shape
    part = width // SPLIT
    n_slot = saved_x.shape[1]
    per_node = n_slot // n_node
    n_hid = w_down.shape[1]
    n_pick = expert_ids.shape[1]
    n_own = SPLIT * per_node
    gate, up, down = w_gate[0].T, w_up[0].T, w_down[0]

    payload = pack(my_node.astype(jnp.int32).reshape(1), out_grad, expert_ids, slot_ids, gate_q, per_node)

    weights = cut_weights(gate, up, down)
    payload, weights = lax.optimization_barrier((payload, weights))
    weights = swap(weights, "node", block)

    here = lax.all_gather(payload, "grp", axis=0, axis_index_groups=along_z, tiled=True)
    there = lax.ppermute(here, "grp", other)
    expert = my_expert.astype(jnp.int32).reshape(1)
    rows, hot_here = select(expert, here, (), 1, n_tok, per_node, n_pick)
    rows, hot_there = select(expert, there, (rows,), n_rest, n_tok, per_node, n_pick)
    rows, weights = lax.optimization_barrier((rows, weights))
    rows = lax.all_to_all(rows, "node", 0, 0, tiled=True)

    gate, rows = lax.optimization_barrier((gate, rows))
    hidden = swap(hidden_part(weights, rows), "node", block)
    hidden = hidden.reshape(SPLIT, n_hid, n_slot)
    coef = forward(saved_x[0], gate, up)
    grads = swap(grads_of(hidden, coef), "node", block)
    parts = lax.all_to_all(slot_part(grads, weights), "node", 0, 0, tiled=True)

    here, there = back_rows(hot_here, hot_there, parts.reshape(n_rest, n_own, part))
    back = total([here, lax.ppermute(there, "grp", other)])
    back = swap(back, "grp", along_z).reshape(n_z, SPLIT * n_tok, part)
    return unpack(back, n_tok)


def solution(mesh):
    in_specs = (
        P(("grp", "node"), None),
        P(("grp", "node"), None),
        P(("grp", "node"), None),
        P(("grp", "node"), None),
        P("grp", None, None),
        P("grp", None, "node"),
        P("grp", None, "node"),
        P("grp", "node", None),
    )
    out_specs = P(("grp", "node"), None)
    return jax.shard_map(local, mesh=mesh, in_specs=in_specs, out_specs=out_specs, check_vma=False)
```

```python
import functools

import jax
import jax.numpy as jnp
from jax import lax
from jax.experimental import pallas as pl
from jax.experimental.pallas import tpu as pltpu
from jax.sharding import PartitionSpec as P

SPLIT = 8
C_DEV = 2
META = 128
VMEM = 48 * 1024 * 1024
f32, bf16 = jnp.float32, jnp.bfloat16


def call(body, out_shape, cost, **kw):
    flops, moved = cost
    return pl.pallas_call(
        body,
        out_shape=out_shape,
        compiler_params=pltpu.CompilerParams(vmem_limit_bytes=VMEM),
        cost_estimate=pl.CostEstimate(
            flops=flops, bytes_accessed=moved, transcendentals=0
        ),
        **kw,
    )


def hbm(*arrays):
    return [pltpu.with_memory_space_constraint(a, pltpu.HBM) for a in arrays]


def swap(a, axis, members):
    return lax.all_to_all(a, axis, 0, 0, axis_index_groups=members, tiled=True)


def total(blocks):
    return functools.reduce(lambda p, q: p + q, [b.astype(f32) for b in blocks]).astype(bf16)


def pack_body(per_node, node_ref, grad_ref, ids_ref, slots_ref, gates_ref, out_ref, held):
    n_tok, n_pick = ids_ref.shape
    part = out_ref.shape[1] - META
    slots = slots_ref[...]
    slots = jnp.where(slots >= 0, slots - node_ref[0] * per_node, -1)
    held[...] = jnp.zeros_like(held)
    grad = grad_ref[...].astype(f32)
    for i in range(SPLIT):
        rows = slice(i * n_tok, (i + 1) * n_tok)
        held[rows, :part] = grad[:, i * part : (i + 1) * part]
        for j, field in enumerate((ids_ref[...], slots, gates_ref[...])):
            held[rows, part + j * n_pick : part + (j + 1) * n_pick] = field.astype(f32)
    out_ref[...] = held[...].astype(bf16)


def pack(node, grad, ids, slots, gates, per_node):
    n_tok, width = grad.shape
    shape = (SPLIT * n_tok, width // SPLIT + META)
    return call(
        functools.partial(pack_body, per_node),
        jax.ShapeDtypeStruct(shape, bf16),
        (0, 4 * n_tok * width),
        in_specs=[pl.BlockSpec(memory_space=pltpu.SMEM)]
        + [pl.BlockSpec(memory_space=pltpu.VMEM)] * 4,
        out_specs=pl.BlockSpec(memory_space=pltpu.VMEM),
        scratch_shapes=[pltpu.VMEM(shape, f32)],
    )(node, grad, ids, slots, gates)


def cut_body(gate_ref, up_ref, down_ref, out_ref, held, sem_in, sem_out):
    n = gate_ref.shape[0]
    part = out_ref.shape[2]
    come = [
        [
            pltpu.make_async_copy(
                ref.at[:, pl.ds(i * part, part)],
                held.at[i, pl.ds(j * n, n)],
                sem_in.at[i, j],
            )
            for j, ref in enumerate((gate_ref, up_ref, down_ref))
        ]
        for i in range(SPLIT)
    ]
    leave = [
        pltpu.make_async_copy(held.at[i], out_ref.at[i], sem_out.at[i])
        for i in range(SPLIT)
    ]
    for copies in come:
        for copy in copies:
            copy.start()
    for i in range(SPLIT):
        for copy in come[i]:
            copy.wait()
        leave[i].start()
    for copy in leave:
        copy.wait()


def cut_weights(gate, up, down):
    n_hid, width = gate.shape
    shape = (SPLIT, 3 * n_hid, width // SPLIT)
    return call(
        cut_body,
        pltpu.HBM(shape, bf16),
        (0, 12 * n_hid * width),
        in_specs=[pl.BlockSpec(memory_space=pl.ANY)] * 3,
        out_specs=pl.BlockSpec(memory_space=pl.ANY),
        scratch_shapes=[
            pltpu.VMEM(shape, bf16),
            pltpu.SemaphoreType.DMA((SPLIT, 3)),
            pltpu.SemaphoreType.DMA((SPLIT,)),
        ],
    )(*hbm(gate, up, down))


def forward_body(x_ref, gate_ref, up_ref, out_ref):
    n = gate_ref.shape[0]
    both = jnp.concatenate([gate_ref[...], up_ref[...]], axis=0)
    pre = lax.dot_general(
        x_ref[...], both, (((1,), (1,)), ((), ())), preferred_element_type=f32
    ).T
    pre_gate, pre_up = pre[:n], pre[n:]
    squash = jax.nn.sigmoid(pre_gate)
    out_ref[:n] = pre_up * squash * (1.0 + pre_gate * (1.0 - squash))
    out_ref[n:] = pre_gate * squash


def forward(x, gate, up):
    n_slot, width = x.shape
    n_hid = gate.shape[0]
    half = n_slot // 2
    spec = pl.BlockSpec((n_hid, width), lambda i: (0, 0))
    return call(
        forward_body,
        jax.ShapeDtypeStruct((2 * n_hid, n_slot), f32),
        (4 * n_hid * n_slot * width, 2 * (n_slot + 2 * n_hid) * width),
        grid=(2,),
        in_specs=[pl.BlockSpec((half, width), lambda i: (i, 0)), spec, spec],
        out_specs=pl.BlockSpec((2 * n_hid, half), lambda i: (0, i)),
    )(*hbm(x, gate, up))


def select_body(n_tok, per_node, n_pick, expert_ref, tok_ref, *refs):
    rows_ref, hot_ref = refs[-2:]
    part = rows_ref.shape[1]
    rout = tok_ref[:, part:].astype(f32)
    lane = lax.broadcasted_iota(jnp.int32, rout.shape, 1)
    row = lax.broadcasted_iota(jnp.int32, rout.shape, 0)
    slot = pltpu.roll(rout, META - n_pick, 1)
    gate = pltpu.roll(rout, META - 2 * n_pick, 1)
    hit = (lane < n_pick) & (rout == expert_ref[0].astype(f32)) & (slot >= 0)
    found = jnp.sum(jnp.where(hit, slot + 1.0, 0.0), axis=1, keepdims=True)
    scale = jnp.sum(jnp.where(hit, gate, 0.0), axis=1, keepdims=True) * (1.0 / 256.0)
    found = found.astype(jnp.int32) - 1
    node = (row // n_tok) % SPLIT
    one_hot = (found >= 0) & (node * per_node + found == lane)
    hot_ref[...] = jnp.where(one_hot, scale, 0.0).astype(bf16)
    pick = jnp.where(one_hot, 1.0, 0.0).T.astype(bf16)
    rows = jnp.dot(pick, tok_ref[:, :part], preferred_element_type=f32).astype(bf16)
    if len(refs) == 3:
        rows = rows + refs[0][...]
    for i in range(rows_ref.shape[0] // rows.shape[0]):
        rows_ref[i * rows.shape[0] : (i + 1) * rows.shape[0]] = rows


def select(expert, tokens, before, copies, n_tok, per_node, n_pick):
    n_all, wide = tokens.shape
    part = wide - META
    n_own = SPLIT * per_node
    return call(
        functools.partial(select_body, n_tok, per_node, n_pick),
        (
            jax.ShapeDtypeStruct((copies * n_own, part), bf16),
            pltpu.HBM((n_all, n_own), bf16),
        ),
        (2 * n_all * n_own * part, 2 * n_all * wide),
        in_specs=[pl.BlockSpec(memory_space=pltpu.SMEM)]
        + [pl.BlockSpec(memory_space=pltpu.VMEM)] * (1 + len(before)),
        out_specs=[pl.BlockSpec(memory_space=pltpu.VMEM)] * 2,
    )(expert, tokens, *before)


def hidden_body(w_ref, rows_ref, out_ref):
    n, h, part = w_ref.shape
    got = lax.dot_general(
        w_ref[...].reshape(n * h, part),
        rows_ref[...],
        (((1,), (1,)), ((), ())),
        preferred_element_type=f32,
    )
    out_ref[...] = got.astype(bf16)


def hidden_part(weights, rows):
    n, h3, part = weights.shape
    h = h3 // 3
    n_slot = rows.shape[0]
    half = n_slot // 2
    return call(
        hidden_body,
        pltpu.HBM((n * h, n_slot), bf16),
        (2 * n * h * n_slot * part, 2 * (n * h + n_slot) * part),
        grid=(2,),
        in_specs=[
            pl.BlockSpec((n, h, part), lambda i: (0, 2, 0)),
            pl.BlockSpec((half, part), lambda i: (i, 0)),
        ],
        out_specs=pl.BlockSpec((n * h, half), lambda i: (0, i)),
    )(weights, rows)


def grads_body(parts_ref, coef_ref, out_ref):
    n, h, _ = parts_ref.shape
    total = jnp.sum(parts_ref[...].astype(f32), axis=0)
    grads = jnp.concatenate([total * coef_ref[:h], total * coef_ref[h:]], axis=0)
    grads = grads.T.astype(bf16)
    for i in range(n):
        out_ref[i] = grads


def grads_of(parts, coef):
    n, h, n_slot = parts.shape
    return call(
        grads_body,
        jax.ShapeDtypeStruct((n, n_slot, 2 * h), bf16),
        (2 * n * h * n_slot, 6 * n * h * n_slot),
    )(parts, coef)


def slot_body(grads_ref, w_ref, out_ref):
    n, h, part = w_ref.shape
    grads = jnp.concatenate([grads_ref[i] for i in range(n)], axis=1)
    got = jnp.dot(grads, w_ref[...].reshape(n * h, part), preferred_element_type=f32)
    out_ref[...] = got.astype(bf16)


def slot_part(grads, weights):
    n, n_slot, h2 = grads.shape
    part = weights.shape[2]
    half = n_slot // 2
    return call(
        slot_body,
        jax.ShapeDtypeStruct((n_slot, part), bf16),
        (2 * n * h2 * n_slot * part, 2 * (n * h2 * (n_slot + part) + n_slot * part)),
        grid=(2,),
        in_specs=[
            pl.BlockSpec((n, half, h2), lambda i: (0, i, 0)),
            pl.BlockSpec((n, h2, part), lambda i: (0, 0, 0)),
        ],
        out_specs=pl.BlockSpec((half, part), lambda i: (i, 0)),
    )(grads, weights)


def back_body(hot_here_ref, hot_there_ref, parts_ref, here_ref, there_ref):
    own = jnp.sum(parts_ref[...].astype(f32), axis=0).astype(bf16)
    for hot_ref, out_ref in ((hot_there_ref, there_ref), (hot_here_ref, here_ref)):
        got = jnp.dot(hot_ref[...], own, preferred_element_type=f32)
        out_ref[...] = got.astype(bf16)


def back_rows(hot_here, hot_there, parts):
    half, n_own = hot_here.shape
    part = parts.shape[2]
    return call(
        back_body,
        (jax.ShapeDtypeStruct((half, part), bf16),) * 2,
        (4 * half * n_own * part, 4 * half * part + 2 * parts.size),
    )(hot_here, hot_there, parts)


def unpack_body(parts_ref, out_ref):
    n_tok = out_ref.shape[0]
    added = jnp.sum(parts_ref[...].astype(f32), axis=0)
    pieces = [added[i * n_tok : (i + 1) * n_tok] for i in range(SPLIT)]
    out_ref[...] = jnp.concatenate(pieces, axis=1).astype(bf16)


def unpack(parts, n_tok):
    return call(
        unpack_body,
        jax.ShapeDtypeStruct((n_tok, SPLIT * parts.shape[2]), bf16),
        (parts.size, 2 * parts.size),
    )(parts)


def local(out_grad, expert_ids, slot_ids, gate_q, saved_x, w_gate, w_up, w_down):
    n_grp, n_node = lax.axis_size("grp"), lax.axis_size("node")
    my_expert, my_node = lax.axis_index("grp"), lax.axis_index("node")
    n_rest, n_z = n_node // SPLIT, n_grp // C_DEV
    block = [[h * SPLIT + d for d in range(SPLIT)] for h in range(n_rest)]
    along_z = [
        [z * C_DEV + (c + z // 2) % C_DEV for z in range(n_z)] for c in range(C_DEV)
    ]
    other = [(z * C_DEV + c, z * C_DEV + 1 - c) for z in range(n_z) for c in range(C_DEV)]
    n_tok, width = out_grad.shape
    part = width // SPLIT
    n_slot = saved_x.shape[1]
    per_node = n_slot // n_node
    n_hid = w_down.shape[1]
    n_pick = expert_ids.shape[1]
    n_own = SPLIT * per_node
    gate, up, down = w_gate[0].T, w_up[0].T, w_down[0]

    payload = pack(my_node.astype(jnp.int32).reshape(1), out_grad, expert_ids, slot_ids, gate_q, per_node)

    weights = cut_weights(gate, up, down)
    payload, weights = lax.optimization_barrier((payload, weights))
    weights = swap(weights, "node", block)

    here = lax.all_gather(payload, "grp", axis=0, axis_index_groups=along_z, tiled=True)
    there, weights = lax.optimization_barrier((lax.ppermute(here, "grp", other), weights))
    expert = my_expert.astype(jnp.int32).reshape(1)
    rows, hot_here = select(expert, here, (), 1, n_tok, per_node, n_pick)
    rows, hot_there = select(expert, there, (rows,), n_rest, n_tok, per_node, n_pick)
    rows = lax.all_to_all(rows, "node", 0, 0, tiled=True)

    gate, rows = lax.optimization_barrier((gate, rows))
    hidden = swap(hidden_part(weights, rows), "node", block)
    hidden = hidden.reshape(SPLIT, n_hid, n_slot)
    coef = forward(saved_x[0], gate, up)
    grads = swap(grads_of(hidden, coef), "node", block)
    parts = lax.all_to_all(slot_part(grads, weights), "node", 0, 0, tiled=True)

    here, there = back_rows(hot_here, hot_there, parts.reshape(n_rest, n_own, part))
    back = total([here, lax.ppermute(there, "grp", other)])
    back = swap(back, "grp", along_z).reshape(n_z, SPLIT * n_tok, part)
    return unpack(back, n_tok)


def solution(mesh):
    in_specs = (
        P(("grp", "node"), None),
        P(("grp", "node"), None),
        P(("grp", "node"), None),
        P(("grp", "node"), None),
        P("grp", None, None),
        P("grp", None, "node"),
        P("grp", None, "node"),
        P("grp", "node", None),
    )
    out_specs = P(("grp", "node"), None)
    return jax.shard_map(local, mesh=mesh, in_specs=in_specs, out_specs=out_specs, check_vma=False)
```

```python
import functools

import jax
import jax.numpy as jnp
from jax import lax
from jax.experimental import pallas as pl
from jax.experimental.pallas import tpu as pltpu
from jax.sharding import PartitionSpec as P

SPLIT = 8
C_DEV = 2
META = 128
VMEM = 48 * 1024 * 1024
f32, bf16 = jnp.float32, jnp.bfloat16


def call(body, out_shape, cost, **kw):
    flops, moved = cost
    return pl.pallas_call(
        body,
        out_shape=out_shape,
        compiler_params=pltpu.CompilerParams(vmem_limit_bytes=VMEM),
        cost_estimate=pl.CostEstimate(
            flops=flops, bytes_accessed=moved, transcendentals=0
        ),
        **kw,
    )


def hbm(*arrays):
    return [pltpu.with_memory_space_constraint(a, pltpu.HBM) for a in arrays]


def swap(a, axis, members):
    return lax.all_to_all(a, axis, 0, 0, axis_index_groups=members, tiled=True)


def total(blocks):
    return functools.reduce(lambda p, q: p + q, [b.astype(f32) for b in blocks]).astype(bf16)


def pack_body(per_node, node_ref, grad_ref, ids_ref, slots_ref, gates_ref, out_ref, held):
    n_tok, n_pick = ids_ref.shape
    part = out_ref.shape[1] - META
    slots = slots_ref[...]
    slots = jnp.where(slots >= 0, slots - node_ref[0] * per_node, -1)
    held[...] = jnp.zeros_like(held)
    grad = grad_ref[...].astype(f32)
    for i in range(SPLIT):
        rows = slice(i * n_tok, (i + 1) * n_tok)
        held[rows, :part] = grad[:, i * part : (i + 1) * part]
        for j, field in enumerate((ids_ref[...], slots, gates_ref[...])):
            held[rows, part + j * n_pick : part + (j + 1) * n_pick] = field.astype(f32)
    out_ref[...] = held[...].astype(bf16)


def pack(node, grad, ids, slots, gates, per_node):
    n_tok, width = grad.shape
    shape = (SPLIT * n_tok, width // SPLIT + META)
    return call(
        functools.partial(pack_body, per_node),
        jax.ShapeDtypeStruct(shape, bf16),
        (0, 4 * n_tok * width),
        in_specs=[pl.BlockSpec(memory_space=pltpu.SMEM)]
        + [pl.BlockSpec(memory_space=pltpu.VMEM)] * 4,
        out_specs=pl.BlockSpec(memory_space=pltpu.VMEM),
        scratch_shapes=[pltpu.VMEM(shape, f32)],
    )(node, grad, ids, slots, gates)


def cut_body(gate_ref, up_ref, down_ref, out_ref, held, sem_in, sem_out):
    n = gate_ref.shape[0]
    part = out_ref.shape[2]
    come = [
        [
            pltpu.make_async_copy(
                ref.at[:, pl.ds(i * part, part)],
                held.at[i, pl.ds(j * n, n)],
                sem_in.at[i, j],
            )
            for j, ref in enumerate((gate_ref, up_ref, down_ref))
        ]
        for i in range(SPLIT)
    ]
    leave = [
        pltpu.make_async_copy(held.at[i], out_ref.at[i], sem_out.at[i])
        for i in range(SPLIT)
    ]
    for copies in come:
        for copy in copies:
            copy.start()
    for i in range(SPLIT):
        for copy in come[i]:
            copy.wait()
        leave[i].start()
    for copy in leave:
        copy.wait()


def cut_weights(gate, up, down):
    n_hid, width = gate.shape
    shape = (SPLIT, 3 * n_hid, width // SPLIT)
    return call(
        cut_body,
        pltpu.HBM(shape, bf16),
        (0, 12 * n_hid * width),
        in_specs=[pl.BlockSpec(memory_space=pl.ANY)] * 3,
        out_specs=pl.BlockSpec(memory_space=pl.ANY),
        scratch_shapes=[
            pltpu.VMEM(shape, bf16),
            pltpu.SemaphoreType.DMA((SPLIT, 3)),
            pltpu.SemaphoreType.DMA((SPLIT,)),
        ],
    )(*hbm(gate, up, down))


def forward_body(x_ref, gate_ref, up_ref, out_ref):
    n = gate_ref.shape[0]
    both = jnp.concatenate([gate_ref[...], up_ref[...]], axis=0)
    pre = lax.dot_general(
        x_ref[...], both, (((1,), (1,)), ((), ())), preferred_element_type=f32
    ).T
    pre_gate, pre_up = pre[:n], pre[n:]
    squash = jax.nn.sigmoid(pre_gate)
    out_ref[:n] = pre_up * squash * (1.0 + pre_gate * (1.0 - squash))
    out_ref[n:] = pre_gate * squash


def forward(x, gate, up):
    n_slot, width = x.shape
    n_hid = gate.shape[0]
    half = n_slot // 2
    spec = pl.BlockSpec((n_hid, width), lambda i: (0, 0))
    return call(
        forward_body,
        jax.ShapeDtypeStruct((2 * n_hid, n_slot), f32),
        (4 * n_hid * n_slot * width, 2 * (n_slot + 2 * n_hid) * width),
        grid=(2,),
        in_specs=[pl.BlockSpec((half, width), lambda i: (i, 0)), spec, spec],
        out_specs=pl.BlockSpec((2 * n_hid, half), lambda i: (0, i)),
    )(*hbm(x, gate, up))


def select_body(n_tok, per_node, n_pick, expert_ref, tok_ref, *refs):
    rows_ref, hot_ref = refs[-2:]
    part = rows_ref.shape[1]
    rout = tok_ref[:, part:].astype(f32)
    lane = lax.broadcasted_iota(jnp.int32, rout.shape, 1)
    row = lax.broadcasted_iota(jnp.int32, rout.shape, 0)
    slot = pltpu.roll(rout, META - n_pick, 1)
    gate = pltpu.roll(rout, META - 2 * n_pick, 1)
    hit = (lane < n_pick) & (rout == expert_ref[0].astype(f32)) & (slot >= 0)
    found = jnp.sum(jnp.where(hit, slot + 1.0, 0.0), axis=1, keepdims=True)
    scale = jnp.sum(jnp.where(hit, gate, 0.0), axis=1, keepdims=True) * (1.0 / 256.0)
    found = found.astype(jnp.int32) - 1
    node = (row // n_tok) % SPLIT
    one_hot = (found >= 0) & (node * per_node + found == lane)
    hot_ref[...] = jnp.where(one_hot, scale, 0.0).astype(bf16)
    pick = jnp.where(one_hot, 1.0, 0.0).T.astype(bf16)
    rows = jnp.dot(pick, tok_ref[:, :part], preferred_element_type=f32).astype(bf16)
    if len(refs) == 3:
        rows = rows + refs[0][...]
    for i in range(rows_ref.shape[0] // rows.shape[0]):
        rows_ref[i * rows.shape[0] : (i + 1) * rows.shape[0]] = rows


def select(expert, tokens, before, copies, n_tok, per_node, n_pick):
    n_all, wide = tokens.shape
    part = wide - META
    n_own = SPLIT * per_node
    return call(
        functools.partial(select_body, n_tok, per_node, n_pick),
        (
            (pltpu.HBM if before else jax.ShapeDtypeStruct)((copies * n_own, part), bf16),
            pltpu.HBM((n_all, n_own), bf16),
        ),
        (2 * n_all * n_own * part, 2 * n_all * wide),
        in_specs=[pl.BlockSpec(memory_space=pltpu.SMEM)]
        + [pl.BlockSpec(memory_space=pltpu.VMEM)] * (1 + len(before)),
        out_specs=[pl.BlockSpec(memory_space=pltpu.VMEM)] * 2,
    )(expert, tokens, *before)


def hidden_body(w_ref, rows_ref, out_ref):
    n, h, part = w_ref.shape
    got = lax.dot_general(
        w_ref[...].reshape(n * h, part),
        rows_ref[...],
        (((1,), (1,)), ((), ())),
        preferred_element_type=f32,
    )
    out_ref[...] = got.astype(bf16)


def hidden_part(weights, rows):
    n, h3, part = weights.shape
    h = h3 // 3
    n_slot = rows.shape[0]
    return call(
        hidden_body,
        pltpu.HBM((n * h, n_slot), bf16),
        (2 * n * h * n_slot * part, 2 * (n * h + n_slot) * part),
        grid=(1,),
        in_specs=[
            pl.BlockSpec((n, h, part), lambda i: (0, 2, 0)),
            pl.BlockSpec((n_slot, part), lambda i: (0, 0)),
        ],
        out_specs=pl.BlockSpec((n * h, n_slot), lambda i: (0, 0)),
    )(weights, rows)


def grads_body(parts_ref, coef_ref, out_ref):
    n, h, _ = parts_ref.shape
    total = jnp.sum(parts_ref[...].astype(f32), axis=0)
    grads = jnp.concatenate([total * coef_ref[:h], total * coef_ref[h:]], axis=0)
    grads = grads.T.astype(bf16)
    for i in range(n):
        out_ref[i] = grads


def grads_of(parts, coef):
    n, h, n_slot = parts.shape
    return call(
        grads_body,
        jax.ShapeDtypeStruct((n, n_slot, 2 * h), bf16),
        (2 * n * h * n_slot, 6 * n * h * n_slot),
    )(parts, coef)


def slot_body(grads_ref, w_ref, out_ref):
    n, h, part = w_ref.shape
    grads = jnp.concatenate([grads_ref[i] for i in range(n)], axis=1)
    got = jnp.dot(grads, w_ref[...].reshape(n * h, part), preferred_element_type=f32)
    out_ref[...] = got.astype(bf16)


def slot_part(grads, weights):
    n, n_slot, h2 = grads.shape
    part = weights.shape[2]
    half = n_slot // 2
    return call(
        slot_body,
        jax.ShapeDtypeStruct((n_slot, part), bf16),
        (2 * n * h2 * n_slot * part, 2 * (n * h2 * (n_slot + part) + n_slot * part)),
        grid=(2,),
        in_specs=[
            pl.BlockSpec((n, half, h2), lambda i: (0, i, 0)),
            pl.BlockSpec((n, h2, part), lambda i: (0, 0, 0)),
        ],
        out_specs=pl.BlockSpec((half, part), lambda i: (i, 0)),
    )(grads, weights)


def back_body(hot_here_ref, hot_there_ref, parts_ref, here_ref, there_ref):
    own = jnp.sum(parts_ref[...].astype(f32), axis=0).astype(bf16)
    for hot_ref, out_ref in ((hot_there_ref, there_ref), (hot_here_ref, here_ref)):
        got = jnp.dot(hot_ref[...], own, preferred_element_type=f32)
        out_ref[...] = got.astype(bf16)


def back_rows(hot_here, hot_there, parts):
    half, n_own = hot_here.shape
    part = parts.shape[2]
    return call(
        back_body,
        (jax.ShapeDtypeStruct((half, part), bf16),) * 2,
        (4 * half * n_own * part, 4 * half * part + 2 * parts.size),
    )(hot_here, hot_there, parts)


def unpack_body(parts_ref, out_ref):
    n_tok = out_ref.shape[0]
    added = jnp.sum(parts_ref[...].astype(f32), axis=0)
    pieces = [added[i * n_tok : (i + 1) * n_tok] for i in range(SPLIT)]
    out_ref[...] = jnp.concatenate(pieces, axis=1).astype(bf16)


def unpack(parts, n_tok):
    return call(
        unpack_body,
        jax.ShapeDtypeStruct((n_tok, SPLIT * parts.shape[2]), bf16),
        (parts.size, 2 * parts.size),
    )(parts)


def local(out_grad, expert_ids, slot_ids, gate_q, saved_x, w_gate, w_up, w_down):
    n_grp, n_node = lax.axis_size("grp"), lax.axis_size("node")
    my_expert, my_node = lax.axis_index("grp"), lax.axis_index("node")
    n_rest, n_z = n_node // SPLIT, n_grp // C_DEV
    block = [[h * SPLIT + d for d in range(SPLIT)] for h in range(n_rest)]
    along_z = [
        [z * C_DEV + (c + z // 2) % C_DEV for z in range(n_z)] for c in range(C_DEV)
    ]
    other = [(z * C_DEV + c, z * C_DEV + 1 - c) for z in range(n_z) for c in range(C_DEV)]
    n_tok, width = out_grad.shape
    part = width // SPLIT
    n_slot = saved_x.shape[1]
    per_node = n_slot // n_node
    n_hid = w_down.shape[1]
    n_pick = expert_ids.shape[1]
    n_own = SPLIT * per_node
    gate, up, down = w_gate[0].T, w_up[0].T, w_down[0]

    payload = pack(my_node.astype(jnp.int32).reshape(1), out_grad, expert_ids, slot_ids, gate_q, per_node)

    weights = cut_weights(gate, up, down)
    payload, weights = lax.optimization_barrier((payload, weights))
    weights = swap(weights, "node", block)

    here = lax.all_gather(payload, "grp", axis=0, axis_index_groups=along_z, tiled=True)
    there = lax.ppermute(here, "grp", other)
    expert = my_expert.astype(jnp.int32).reshape(1)
    rows, hot_here = select(expert, here, (), 1, n_tok, per_node, n_pick)
    rows, hot_there = select(expert, there, (rows,), n_rest, n_tok, per_node, n_pick)
    rows, weights = lax.optimization_barrier((rows, weights))
    rows = lax.all_to_all(rows, "node", 0, 0, tiled=True)

    gate, rows = lax.optimization_barrier((gate, rows))
    hidden = swap(hidden_part(weights, rows), "node", block)
    hidden = hidden.reshape(SPLIT, n_hid, n_slot)
    coef = forward(saved_x[0], gate, up)
    grads = swap(grads_of(hidden, coef), "node", block)
    parts = lax.all_to_all(slot_part(grads, weights), "node", 0, 0, tiled=True)

    here, there = back_rows(hot_here, hot_there, parts.reshape(n_rest, n_own, part))
    back = total([here, lax.ppermute(there, "grp", other)])
    back = swap(back, "grp", along_z).reshape(n_z, SPLIT * n_tok, part)
    return unpack(back, n_tok)


def solution(mesh):
    in_specs = (
        P(("grp", "node"), None),
        P(("grp", "node"), None),
        P(("grp", "node"), None),
        P(("grp", "node"), None),
        P("grp", None, None),
        P("grp", None, "node"),
        P("grp", None, "node"),
        P("grp", "node", None),
    )
    out_specs = P(("grp", "node"), None)
    return jax.shard_map(local, mesh=mesh, in_specs=in_specs, out_specs=out_specs, check_vma=False)
```

```python
import functools

import jax
import jax.numpy as jnp
from jax import lax
from jax.experimental import pallas as pl
from jax.experimental.pallas import tpu as pltpu
from jax.sharding import PartitionSpec as P

SPLIT = 8
C_DEV = 2
ROWS_AT_ONCE = 128
META = 128
VMEM = 48 * 1024 * 1024
f32, bf16 = jnp.float32, jnp.bfloat16


def call(body, out_shape, cost, **kw):
    flops, moved = cost
    return pl.pallas_call(
        body,
        out_shape=out_shape,
        compiler_params=pltpu.CompilerParams(vmem_limit_bytes=VMEM),
        cost_estimate=pl.CostEstimate(
            flops=flops, bytes_accessed=moved, transcendentals=0
        ),
        **kw,
    )


def hbm(*arrays):
    return [pltpu.with_memory_space_constraint(a, pltpu.HBM) for a in arrays]


def swap(a, axis, members):
    return lax.all_to_all(a, axis, 0, 0, axis_index_groups=members, tiled=True)


def total(blocks):
    return functools.reduce(lambda p, q: p + q, [b.astype(f32) for b in blocks]).astype(bf16)


def pack_body(per_node, node_ref, grad_ref, ids_ref, slots_ref, gates_ref, out_ref, held):
    n_tok, n_pick = ids_ref.shape
    part = out_ref.shape[1] - META
    slots = slots_ref[...]
    slots = jnp.where(slots >= 0, slots - node_ref[0] * per_node, -1)
    held[...] = jnp.zeros_like(held)
    grad = grad_ref[...].astype(f32)
    for i in range(SPLIT):
        rows = slice(i * n_tok, (i + 1) * n_tok)
        held[rows, :part] = grad[:, i * part : (i + 1) * part]
        for j, field in enumerate((ids_ref[...], slots, gates_ref[...])):
            held[rows, part + j * n_pick : part + (j + 1) * n_pick] = field.astype(f32)
    out_ref[...] = held[...].astype(bf16)


def pack(node, grad, ids, slots, gates, per_node):
    n_tok, width = grad.shape
    shape = (SPLIT * n_tok, width // SPLIT + META)
    return call(
        functools.partial(pack_body, per_node),
        jax.ShapeDtypeStruct(shape, bf16),
        (0, 4 * n_tok * width),
        in_specs=[pl.BlockSpec(memory_space=pltpu.SMEM)]
        + [pl.BlockSpec(memory_space=pltpu.VMEM)] * 4,
        out_specs=pl.BlockSpec(memory_space=pltpu.VMEM),
        scratch_shapes=[pltpu.VMEM(shape, f32)],
    )(node, grad, ids, slots, gates)


def cut_body(gate_ref, up_ref, down_ref, out_ref, held, sem_in, sem_out):
    n = gate_ref.shape[0]
    part = out_ref.shape[2]
    come = [
        [
            pltpu.make_async_copy(
                ref.at[:, pl.ds(i * part, part)],
                held.at[i, pl.ds(j * n, n)],
                sem_in.at[i, j],
            )
            for j, ref in enumerate((gate_ref, up_ref, down_ref))
        ]
        for i in range(SPLIT)
    ]
    leave = [
        pltpu.make_async_copy(held.at[i], out_ref.at[i], sem_out.at[i])
        for i in range(SPLIT)
    ]
    for copies in come:
        for copy in copies:
            copy.start()
    for i in range(SPLIT):
        for copy in come[i]:
            copy.wait()
        leave[i].start()
    for copy in leave:
        copy.wait()


def cut_weights(gate, up, down):
    n_hid, width = gate.shape
    shape = (SPLIT, 3 * n_hid, width // SPLIT)
    return call(
        cut_body,
        pltpu.HBM(shape, bf16),
        (0, 12 * n_hid * width),
        in_specs=[pl.BlockSpec(memory_space=pl.ANY)] * 3,
        out_specs=pl.BlockSpec(memory_space=pl.ANY),
        scratch_shapes=[
            pltpu.VMEM(shape, bf16),
            pltpu.SemaphoreType.DMA((SPLIT, 3)),
            pltpu.SemaphoreType.DMA((SPLIT,)),
        ],
    )(*hbm(gate, up, down))


def forward_body(run_ref, x_ref, gate_ref, up_ref, *refs):
    done_ref = refs[0] if len(refs) == 6 else None
    out_ref, held_x, held_w, sem_x, sem_w = refs[-5:]
    n = gate_ref.shape[0]
    n_slot = x_ref.shape[0]
    rows = n_slot // sem_x.shape[0]
    block = ROWS_AT_ONCE

    @pl.when(run_ref[0] != 0)
    def _():
        weights = [
            pltpu.make_async_copy(ref, held_w.at[pl.ds(j * n, n)], sem_w.at[j])
            for j, ref in enumerate((gate_ref, up_ref))
        ]
        inputs = [
            pltpu.make_async_copy(
                x_ref.at[pl.ds(i * rows, rows)],
                held_x.at[pl.ds(i * rows, rows)],
                sem_x.at[i],
            )
            for i in range(n_slot // rows)
        ]
        for copy in weights + inputs:
            copy.start()
        for copy in weights:
            copy.wait()
        for start in range(0, n_slot, block):
            for i in range(start // rows, (start + block) // rows):
                inputs[i].wait()
            pre = lax.dot_general(
                held_w[...],
                held_x[start : start + block],
                (((1,), (1,)), ((), ())),
                preferred_element_type=f32,
            )
            pre_gate, pre_up = pre[:n], pre[n:]
            squash = jax.nn.sigmoid(pre_gate)
            out_ref[:n, start : start + block] = (
                pre_up * squash * (1.0 + pre_gate * (1.0 - squash))
            )
            out_ref[n:, start : start + block] = pre_gate * squash

    @pl.when(run_ref[0] == 0)
    def _():
        out_ref[...] = jnp.zeros_like(out_ref) if done_ref is None else done_ref[...]


def forward(run, x, gate, up, *done):
    n_slot, width = x.shape
    n_hid = gate.shape[0]
    return call(
        forward_body,
        jax.ShapeDtypeStruct((2 * n_hid, n_slot), f32),
        (4 * n_hid * n_slot * width, 2 * (n_slot + 2 * n_hid) * width),
        in_specs=[pl.BlockSpec(memory_space=pltpu.SMEM)]
        + [pl.BlockSpec(memory_space=pl.ANY)] * 3
        + [pl.BlockSpec(memory_space=pltpu.VMEM)] * len(done),
        out_specs=pl.BlockSpec(memory_space=pltpu.VMEM),
        scratch_shapes=[
            pltpu.VMEM((n_slot, width), bf16),
            pltpu.VMEM((2 * n_hid, width), bf16),
            pltpu.SemaphoreType.DMA((16,)),
            pltpu.SemaphoreType.DMA((2,)),
        ],
    )(run, *hbm(x, gate, up), *done)


def select_body(n_tok, per_node, n_pick, expert_ref, tok_ref, *refs):
    rows_ref, hot_ref = refs[-2:]
    part = rows_ref.shape[1]
    rout = tok_ref[:, part:].astype(f32)
    lane = lax.broadcasted_iota(jnp.int32, rout.shape, 1)
    row = lax.broadcasted_iota(jnp.int32, rout.shape, 0)
    slot = pltpu.roll(rout, META - n_pick, 1)
    gate = pltpu.roll(rout, META - 2 * n_pick, 1)
    hit = (lane < n_pick) & (rout == expert_ref[0].astype(f32)) & (slot >= 0)
    found = jnp.sum(jnp.where(hit, slot + 1.0, 0.0), axis=1, keepdims=True)
    scale = jnp.sum(jnp.where(hit, gate, 0.0), axis=1, keepdims=True) * (1.0 / 256.0)
    found = found.astype(jnp.int32) - 1
    node = (row // n_tok) % SPLIT
    one_hot = (found >= 0) & (node * per_node + found == lane)
    hot_ref[...] = jnp.where(one_hot, scale, 0.0).astype(bf16)
    pick = jnp.where(one_hot, 1.0, 0.0).T.astype(bf16)
    rows = jnp.dot(pick, tok_ref[:, :part], preferred_element_type=f32).astype(bf16)
    if len(refs) == 3:
        rows = rows + refs[0][...]
    for i in range(rows_ref.shape[0] // rows.shape[0]):
        rows_ref[i * rows.shape[0] : (i + 1) * rows.shape[0]] = rows


def select(expert, tokens, before, copies, n_tok, per_node, n_pick):
    n_all, wide = tokens.shape
    part = wide - META
    n_own = SPLIT * per_node
    return call(
        functools.partial(select_body, n_tok, per_node, n_pick),
        (
            (pltpu.HBM if before else jax.ShapeDtypeStruct)((copies * n_own, part), bf16),
            pltpu.HBM((n_all, n_own), bf16),
        ),
        (2 * n_all * n_own * part, 2 * n_all * wide),
        in_specs=[pl.BlockSpec(memory_space=pltpu.SMEM)]
        + [pl.BlockSpec(memory_space=pltpu.VMEM)] * (1 + len(before)),
        out_specs=[pl.BlockSpec(memory_space=pltpu.VMEM)] * 2,
    )(expert, tokens, *before)


def hidden_body(w_ref, rows_ref, out_ref):
    n, h, part = w_ref.shape
    got = lax.dot_general(
        w_ref[...].reshape(n * h, part),
        rows_ref[...],
        (((1,), (1,)), ((), ())),
        preferred_element_type=f32,
    )
    out_ref[...] = got.astype(bf16)


def hidden_part(weights, rows):
    n, h3, part = weights.shape
    h = h3 // 3
    n_slot = rows.shape[0]
    return call(
        hidden_body,
        pltpu.HBM((n * h, n_slot), bf16),
        (2 * n * h * n_slot * part, 2 * (n * h + n_slot) * part),
        grid=(1,),
        in_specs=[
            pl.BlockSpec((n, h, part), lambda i: (0, 2, 0)),
            pl.BlockSpec((n_slot, part), lambda i: (0, 0)),
        ],
        out_specs=pl.BlockSpec((n * h, n_slot), lambda i: (0, 0)),
    )(weights, rows)


def grads_body(parts_ref, coef_ref, out_ref):
    n, h, _ = parts_ref.shape
    total = jnp.sum(parts_ref[...].astype(f32), axis=0)
    grads = jnp.concatenate([total * coef_ref[:h], total * coef_ref[h:]], axis=0)
    grads = grads.T.astype(bf16)
    for i in range(n):
        out_ref[i] = grads


def grads_of(parts, coef):
    n, h, n_slot = parts.shape
    return call(
        grads_body,
        jax.ShapeDtypeStruct((n, n_slot, 2 * h), bf16),
        (2 * n * h * n_slot, 6 * n * h * n_slot),
    )(parts, coef)


def slot_body(grads_ref, w_ref, out_ref):
    n, h, part = w_ref.shape
    grads = jnp.concatenate([grads_ref[i] for i in range(n)], axis=1)
    got = jnp.dot(grads, w_ref[...].reshape(n * h, part), preferred_element_type=f32)
    out_ref[...] = got.astype(bf16)


def slot_part(grads, weights):
    n, n_slot, h2 = grads.shape
    part = weights.shape[2]
    half = n_slot // 2
    return call(
        slot_body,
        jax.ShapeDtypeStruct((n_slot, part), bf16),
        (2 * n * h2 * n_slot * part, 2 * (n * h2 * (n_slot + part) + n_slot * part)),
        grid=(2,),
        in_specs=[
            pl.BlockSpec((n, half, h2), lambda i: (0, i, 0)),
            pl.BlockSpec((n, h2, part), lambda i: (0, 0, 0)),
        ],
        out_specs=pl.BlockSpec((half, part), lambda i: (i, 0)),
    )(grads, weights)


def back_body(hot_here_ref, hot_there_ref, parts_ref, here_ref, there_ref):
    own = jnp.sum(parts_ref[...].astype(f32), axis=0).astype(bf16)
    for hot_ref, out_ref in ((hot_there_ref, there_ref), (hot_here_ref, here_ref)):
        got = jnp.dot(hot_ref[...], own, preferred_element_type=f32)
        out_ref[...] = got.astype(bf16)


def back_rows(hot_here, hot_there, parts):
    half, n_own = hot_here.shape
    part = parts.shape[2]
    return call(
        back_body,
        (jax.ShapeDtypeStruct((half, part), bf16),) * 2,
        (4 * half * n_own * part, 4 * half * part + 2 * parts.size),
    )(hot_here, hot_there, parts)


def unpack_body(parts_ref, out_ref):
    n_tok = out_ref.shape[0]
    added = jnp.sum(parts_ref[...].astype(f32), axis=0)
    pieces = [added[i * n_tok : (i + 1) * n_tok] for i in range(SPLIT)]
    out_ref[...] = jnp.concatenate(pieces, axis=1).astype(bf16)


def unpack(parts, n_tok):
    return call(
        unpack_body,
        jax.ShapeDtypeStruct((n_tok, SPLIT * parts.shape[2]), bf16),
        (parts.size, 2 * parts.size),
    )(parts)


def local(out_grad, expert_ids, slot_ids, gate_q, saved_x, w_gate, w_up, w_down):
    n_grp, n_node = lax.axis_size("grp"), lax.axis_size("node")
    my_expert, my_node = lax.axis_index("grp"), lax.axis_index("node")
    n_rest, n_z = n_node // SPLIT, n_grp // C_DEV
    block = [[h * SPLIT + d for d in range(SPLIT)] for h in range(n_rest)]
    along_z = [
        [z * C_DEV + (c + z // 2) % C_DEV for z in range(n_z)] for c in range(C_DEV)
    ]
    other = [(z * C_DEV + c, z * C_DEV + 1 - c) for z in range(n_z) for c in range(C_DEV)]
    n_tok, width = out_grad.shape
    part = width // SPLIT
    n_slot = saved_x.shape[1]
    per_node = n_slot // n_node
    n_hid = w_down.shape[1]
    n_pick = expert_ids.shape[1]
    n_own = SPLIT * per_node
    gate, up, down = w_gate[0].T, w_up[0].T, w_down[0]

    payload = pack(my_node.astype(jnp.int32).reshape(1), out_grad, expert_ids, slot_ids, gate_q, per_node)

    weights = cut_weights(gate, up, down)
    payload, weights = lax.optimization_barrier((payload, weights))
    weights = swap(weights, "node", block)

    here = lax.all_gather(payload, "grp", axis=0, axis_index_groups=along_z, tiled=True)
    there = lax.ppermute(here, "grp", other)
    expert = my_expert.astype(jnp.int32).reshape(1)
    rows, hot_here = select(expert, here, (), 1, n_tok, per_node, n_pick)
    rows, hot_there = select(expert, there, (rows,), n_rest, n_tok, per_node, n_pick)
    late = (my_expert % C_DEV).astype(jnp.int32).reshape(1)
    gate, rows = lax.optimization_barrier((gate, rows))
    coef = forward(late, saved_x[0], gate, up)
    rows, weights, coef = lax.optimization_barrier((rows, weights, coef))
    rows = lax.all_to_all(rows, "node", 0, 0, tiled=True)

    gate, rows = lax.optimization_barrier((gate, rows))
    hidden = swap(hidden_part(weights, rows), "node", block)
    hidden = hidden.reshape(SPLIT, n_hid, n_slot)
    coef = forward(1 - late, saved_x[0], gate, up, coef)
    grads = swap(grads_of(hidden, coef), "node", block)
    parts = lax.all_to_all(slot_part(grads, weights), "node", 0, 0, tiled=True)

    here, there = back_rows(hot_here, hot_there, parts.reshape(n_rest, n_own, part))
    back = total([here, lax.ppermute(there, "grp", other)])
    back = swap(back, "grp", along_z).reshape(n_z, SPLIT * n_tok, part)
    return unpack(back, n_tok)


def solution(mesh):
    in_specs = (
        P(("grp", "node"), None),
        P(("grp", "node"), None),
        P(("grp", "node"), None),
        P(("grp", "node"), None),
        P("grp", None, None),
        P("grp", None, "node"),
        P("grp", None, "node"),
        P("grp", "node", None),
    )
    out_specs = P(("grp", "node"), None)
    return jax.shard_map(local, mesh=mesh, in_specs=in_specs, out_specs=out_specs, check_vma=False)
```

```python
import functools

import jax
import jax.numpy as jnp
from jax import lax
from jax.experimental import pallas as pl
from jax.experimental.pallas import tpu as pltpu
from jax.sharding import PartitionSpec as P

SPLIT = 8
C_DEV = 2
BLOCK = 128
META = 128
VMEM = 48 * 1024 * 1024
f32, bf16 = jnp.float32, jnp.bfloat16


def call(body, out_shape, cost, **kw):
    flops, moved = cost
    return pl.pallas_call(
        body,
        out_shape=out_shape,
        compiler_params=pltpu.CompilerParams(vmem_limit_bytes=VMEM),
        cost_estimate=pl.CostEstimate(
            flops=flops, bytes_accessed=moved, transcendentals=0
        ),
        **kw,
    )


def hbm(*arrays):
    return [pltpu.with_memory_space_constraint(a, pltpu.HBM) for a in arrays]


def swap(a, axis, members):
    return lax.all_to_all(a, axis, 0, 0, axis_index_groups=members, tiled=True)


def total(blocks):
    return functools.reduce(lambda p, q: p + q, [b.astype(f32) for b in blocks]).astype(bf16)


def pack_body(per_node, node_ref, grad_ref, ids_ref, slots_ref, gates_ref, out_ref, held):
    n_tok, n_pick = ids_ref.shape
    part = out_ref.shape[1] - META
    slots = slots_ref[...]
    slots = jnp.where(slots >= 0, slots - node_ref[0] * per_node, -1)
    held[...] = jnp.zeros_like(held)
    grad = grad_ref[...].astype(f32)
    for i in range(SPLIT):
        rows = slice(i * n_tok, (i + 1) * n_tok)
        held[rows, :part] = grad[:, i * part : (i + 1) * part]
        for j, field in enumerate((ids_ref[...], slots, gates_ref[...])):
            held[rows, part + j * n_pick : part + (j + 1) * n_pick] = field.astype(f32)
    out_ref[...] = held[...].astype(bf16)


def pack(node, grad, ids, slots, gates, per_node):
    n_tok, width = grad.shape
    shape = (SPLIT * n_tok, width // SPLIT + META)
    return call(
        functools.partial(pack_body, per_node),
        jax.ShapeDtypeStruct(shape, bf16),
        (0, 4 * n_tok * width),
        in_specs=[pl.BlockSpec(memory_space=pltpu.SMEM)]
        + [pl.BlockSpec(memory_space=pltpu.VMEM)] * 4,
        out_specs=pl.BlockSpec(memory_space=pltpu.VMEM),
        scratch_shapes=[pltpu.VMEM(shape, f32)],
    )(node, grad, ids, slots, gates)


def cut_body(gate_ref, up_ref, down_ref, out_ref, held, sem_in, sem_out):
    n = gate_ref.shape[0]
    part = out_ref.shape[2]
    come = [
        [
            pltpu.make_async_copy(
                ref.at[:, pl.ds(i * part, part)],
                held.at[i, pl.ds(j * n, n)],
                sem_in.at[i, j],
            )
            for j, ref in enumerate((gate_ref, up_ref, down_ref))
        ]
        for i in range(SPLIT)
    ]
    leave = [
        pltpu.make_async_copy(held.at[i], out_ref.at[i], sem_out.at[i])
        for i in range(SPLIT)
    ]
    for copies in come:
        for copy in copies:
            copy.start()
    for i in range(SPLIT):
        for copy in come[i]:
            copy.wait()
        leave[i].start()
    for copy in leave:
        copy.wait()


def cut_weights(gate, up, down):
    n_hid, width = gate.shape
    shape = (SPLIT, 3 * n_hid, width // SPLIT)
    return call(
        cut_body,
        pltpu.HBM(shape, bf16),
        (0, 12 * n_hid * width),
        in_specs=[pl.BlockSpec(memory_space=pl.ANY)] * 3,
        out_specs=pl.BlockSpec(memory_space=pl.ANY),
        scratch_shapes=[
            pltpu.VMEM(shape, bf16),
            pltpu.SemaphoreType.DMA((SPLIT, 3)),
            pltpu.SemaphoreType.DMA((SPLIT,)),
        ],
    )(*hbm(gate, up, down))


def coefficients(pre_gate, pre_up):
    squash = jax.nn.sigmoid(pre_gate)
    return pre_up * squash * (1.0 + pre_gate * (1.0 - squash)), pre_gate * squash


def early_body(run_ref, x_ref, gate_ref, up_ref, out_ref, held_x, held_w, sem_x, sem_w):
    n = gate_ref.shape[0]
    n_slot = x_ref.shape[0]
    rows = n_slot // sem_x.shape[0]

    @pl.when(run_ref[0] != 0)
    def _():
        weights = [
            pltpu.make_async_copy(ref, held_w.at[j], sem_w.at[j])
            for j, ref in enumerate((gate_ref, up_ref))
        ]
        inputs = [
            pltpu.make_async_copy(
                x_ref.at[pl.ds(i * rows, rows)],
                held_x.at[pl.ds(i * rows, rows)],
                sem_x.at[i],
            )
            for i in range(n_slot // rows)
        ]
        for copy in weights + inputs:
            copy.start()
        for copy in weights:
            copy.wait()
        for start in range(0, n_slot, BLOCK):
            for i in range(start // rows, (start + BLOCK) // rows):
                inputs[i].wait()
            pre_gate, pre_up = (
                lax.dot_general(
                    held_w[j],
                    held_x[start : start + BLOCK],
                    (((1,), (1,)), ((), ())),
                    preferred_element_type=f32,
                )
                for j in range(2)
            )
            for j, value in enumerate(coefficients(pre_gate, pre_up)):
                out_ref[j * n : (j + 1) * n, start : start + BLOCK] = value

    @pl.when(run_ref[0] == 0)
    def _():
        out_ref[...] = jnp.zeros_like(out_ref)


def early_forward(run, x, gate, up):
    n_slot, width = x.shape
    n_hid = gate.shape[0]
    return call(
        early_body,
        jax.ShapeDtypeStruct((2 * n_hid, n_slot), f32),
        (4 * n_hid * n_slot * width, 2 * (n_slot + 2 * n_hid) * width),
        in_specs=[pl.BlockSpec(memory_space=pltpu.SMEM)]
        + [pl.BlockSpec(memory_space=pl.ANY)] * 3,
        out_specs=pl.BlockSpec(memory_space=pltpu.VMEM),
        scratch_shapes=[
            pltpu.VMEM((n_slot, width), bf16),
            pltpu.VMEM((2, n_hid, width), bf16),
            pltpu.SemaphoreType.DMA((16,)),
            pltpu.SemaphoreType.DMA((2,)),
        ],
    )(run, *hbm(x, gate, up))


def late_body(run_ref, x_ref, gate_ref, up_ref, done_ref, out_ref):
    n = gate_ref.shape[0]

    @pl.when(run_ref[0] != 0)
    def _():
        both = jnp.concatenate([gate_ref[...], up_ref[...]], axis=0)
        pre = lax.dot_general(
            x_ref[...], both, (((1,), (1,)), ((), ())), preferred_element_type=f32
        ).T
        for j, value in enumerate(coefficients(pre[:n], pre[n:])):
            out_ref[j * n : (j + 1) * n] = value

    @pl.when(run_ref[0] == 0)
    def _():
        out_ref[...] = done_ref[...]


def late_forward(run, x, gate, up, done):
    n_slot, width = x.shape
    n_hid = gate.shape[0]
    half = n_slot // 2
    spec = pl.BlockSpec((n_hid, width), lambda i: (0, 0))
    out = pl.BlockSpec((2 * n_hid, half), lambda i: (0, i))
    return call(
        late_body,
        pltpu.HBM((2 * n_hid, n_slot), f32),
        (4 * n_hid * n_slot * width, 2 * (n_slot + 2 * n_hid) * width),
        grid=(2,),
        in_specs=[
            pl.BlockSpec(memory_space=pltpu.SMEM),
            pl.BlockSpec((half, width), lambda i: (i, 0)),
            spec,
            spec,
            out,
        ],
        out_specs=out,
    )(run, *hbm(x, gate, up), done)


def select_body(n_tok, per_node, n_pick, expert_ref, tok_ref, *refs):
    rows_ref, hot_ref = refs[-2:]
    part = rows_ref.shape[1]
    rout = tok_ref[:, part:].astype(f32)
    lane = lax.broadcasted_iota(jnp.int32, rout.shape, 1)
    row = lax.broadcasted_iota(jnp.int32, rout.shape, 0)
    slot = pltpu.roll(rout, META - n_pick, 1)
    gate = pltpu.roll(rout, META - 2 * n_pick, 1)
    hit = (lane < n_pick) & (rout == expert_ref[0].astype(f32)) & (slot >= 0)
    found = jnp.sum(jnp.where(hit, slot + 1.0, 0.0), axis=1, keepdims=True)
    scale = jnp.sum(jnp.where(hit, gate, 0.0), axis=1, keepdims=True) * (1.0 / 256.0)
    found = found.astype(jnp.int32) - 1
    node = (row // n_tok) % SPLIT
    one_hot = (found >= 0) & (node * per_node + found == lane)
    hot_ref[...] = jnp.where(one_hot, scale, 0.0).astype(bf16)
    pick = jnp.where(one_hot, 1.0, 0.0).T.astype(bf16)
    rows = jnp.dot(pick, tok_ref[:, :part], preferred_element_type=f32).astype(bf16)
    if len(refs) == 3:
        rows = rows + refs[0][...]
    for i in range(rows_ref.shape[0] // rows.shape[0]):
        rows_ref[i * rows.shape[0] : (i + 1) * rows.shape[0]] = rows


def select(expert, tokens, before, copies, n_tok, per_node, n_pick):
    n_all, wide = tokens.shape
    part = wide - META
    n_own = SPLIT * per_node
    return call(
        functools.partial(select_body, n_tok, per_node, n_pick),
        (
            (pltpu.HBM if before else jax.ShapeDtypeStruct)((copies * n_own, part), bf16),
            pltpu.HBM((n_all, n_own), bf16),
        ),
        (2 * n_all * n_own * part, 2 * n_all * wide),
        in_specs=[pl.BlockSpec(memory_space=pltpu.SMEM)]
        + [pl.BlockSpec(memory_space=pltpu.VMEM)] * (1 + len(before)),
        out_specs=[pl.BlockSpec(memory_space=pltpu.VMEM)] * 2,
    )(expert, tokens, *before)


def hidden_body(w_ref, rows_ref, out_ref):
    n, h, part = w_ref.shape
    got = lax.dot_general(
        w_ref[...].reshape(n * h, part),
        rows_ref[...],
        (((1,), (1,)), ((), ())),
        preferred_element_type=f32,
    )
    out_ref[...] = got.astype(bf16)


def hidden_part(weights, rows):
    n, h3, part = weights.shape
    h = h3 // 3
    n_slot = rows.shape[0]
    return call(
        hidden_body,
        pltpu.HBM((n * h, n_slot), bf16),
        (2 * n * h * n_slot * part, 2 * (n * h + n_slot) * part),
        grid=(1,),
        in_specs=[
            pl.BlockSpec((n, h, part), lambda i: (0, 2, 0)),
            pl.BlockSpec((n_slot, part), lambda i: (0, 0)),
        ],
        out_specs=pl.BlockSpec((n * h, n_slot), lambda i: (0, 0)),
    )(weights, rows)


def grads_body(parts_ref, coef_ref, out_ref):
    n, h, _ = parts_ref.shape
    total = jnp.sum(parts_ref[...].astype(f32), axis=0)
    grads = jnp.concatenate([total * coef_ref[:h], total * coef_ref[h:]], axis=0)
    grads = grads.T.astype(bf16)
    for i in range(n):
        out_ref[i] = grads


def grads_of(parts, coef):
    n, h, n_slot = parts.shape
    return call(
        grads_body,
        jax.ShapeDtypeStruct((n, n_slot, 2 * h), bf16),
        (2 * n * h * n_slot, 6 * n * h * n_slot),
    )(parts, *hbm(coef))


def slot_body(grads_ref, w_ref, out_ref):
    n, h, part = w_ref.shape
    grads = jnp.concatenate([grads_ref[i] for i in range(n)], axis=1)
    got = jnp.dot(grads, w_ref[...].reshape(n * h, part), preferred_element_type=f32)
    out_ref[...] = got.astype(bf16)


def slot_part(grads, weights):
    n, n_slot, h2 = grads.shape
    part = weights.shape[2]
    half = n_slot // 2
    return call(
        slot_body,
        jax.ShapeDtypeStruct((n_slot, part), bf16),
        (2 * n * h2 * n_slot * part, 2 * (n * h2 * (n_slot + part) + n_slot * part)),
        grid=(2,),
        in_specs=[
            pl.BlockSpec((n, half, h2), lambda i: (0, i, 0)),
            pl.BlockSpec((n, h2, part), lambda i: (0, 0, 0)),
        ],
        out_specs=pl.BlockSpec((half, part), lambda i: (i, 0)),
    )(grads, weights)


def back_body(hot_here_ref, hot_there_ref, parts_ref, here_ref, there_ref):
    own = jnp.sum(parts_ref[...].astype(f32), axis=0).astype(bf16)
    for hot_ref, out_ref in ((hot_there_ref, there_ref), (hot_here_ref, here_ref)):
        got = jnp.dot(hot_ref[...], own, preferred_element_type=f32)
        out_ref[...] = got.astype(bf16)


def back_rows(hot_here, hot_there, parts):
    half, n_own = hot_here.shape
    part = parts.shape[2]
    return call(
        back_body,
        (jax.ShapeDtypeStruct((half, part), bf16),) * 2,
        (4 * half * n_own * part, 4 * half * part + 2 * parts.size),
    )(hot_here, hot_there, parts)


def unpack_body(parts_ref, out_ref):
    n_tok = out_ref.shape[0]
    added = jnp.sum(parts_ref[...].astype(f32), axis=0)
    pieces = [added[i * n_tok : (i + 1) * n_tok] for i in range(SPLIT)]
    out_ref[...] = jnp.concatenate(pieces, axis=1).astype(bf16)


def unpack(parts, n_tok):
    return call(
        unpack_body,
        jax.ShapeDtypeStruct((n_tok, SPLIT * parts.shape[2]), bf16),
        (parts.size, 2 * parts.size),
    )(parts)


def local(out_grad, expert_ids, slot_ids, gate_q, saved_x, w_gate, w_up, w_down):
    n_grp, n_node = lax.axis_size("grp"), lax.axis_size("node")
    my_expert, my_node = lax.axis_index("grp"), lax.axis_index("node")
    n_rest, n_z = n_node // SPLIT, n_grp // C_DEV
    block = [[h * SPLIT + d for d in range(SPLIT)] for h in range(n_rest)]
    along_z = [
        [z * C_DEV + (c + z // 2) % C_DEV for z in range(n_z)] for c in range(C_DEV)
    ]
    other = [(z * C_DEV + c, z * C_DEV + 1 - c) for z in range(n_z) for c in range(C_DEV)]
    n_tok, width = out_grad.shape
    part = width // SPLIT
    n_slot = saved_x.shape[1]
    per_node = n_slot // n_node
    n_hid = w_down.shape[1]
    n_pick = expert_ids.shape[1]
    n_own = SPLIT * per_node
    gate, up, down = w_gate[0].T, w_up[0].T, w_down[0]

    payload = pack(my_node.astype(jnp.int32).reshape(1), out_grad, expert_ids, slot_ids, gate_q, per_node)

    weights = cut_weights(gate, up, down)
    payload, weights = lax.optimization_barrier((payload, weights))
    weights = swap(weights, "node", block)

    here = lax.all_gather(payload, "grp", axis=0, axis_index_groups=along_z, tiled=True)
    there = lax.ppermute(here, "grp", other)
    expert = my_expert.astype(jnp.int32).reshape(1)
    rows, hot_here = select(expert, here, (), 1, n_tok, per_node, n_pick)
    rows, hot_there = select(expert, there, (rows,), n_rest, n_tok, per_node, n_pick)
    late = (my_expert % C_DEV).astype(jnp.int32).reshape(1)
    gate, rows = lax.optimization_barrier((gate, rows))
    coef = early_forward(late, saved_x[0], gate, up)
    rows, weights, coef = lax.optimization_barrier((rows, weights, coef))
    rows = lax.all_to_all(rows, "node", 0, 0, tiled=True)

    gate, rows = lax.optimization_barrier((gate, rows))
    hidden = swap(hidden_part(weights, rows), "node", block)
    hidden = hidden.reshape(SPLIT, n_hid, n_slot)
    coef = late_forward(1 - late, saved_x[0], gate, up, coef)
    grads = swap(grads_of(hidden, coef), "node", block)
    parts = lax.all_to_all(slot_part(grads, weights), "node", 0, 0, tiled=True)

    here, there = back_rows(hot_here, hot_there, parts.reshape(n_rest, n_own, part))
    back = total([here, lax.ppermute(there, "grp", other)])
    back = swap(back, "grp", along_z).reshape(n_z, SPLIT * n_tok, part)
    return unpack(back, n_tok)


def solution(mesh):
    in_specs = (
        P(("grp", "node"), None),
        P(("grp", "node"), None),
        P(("grp", "node"), None),
        P(("grp", "node"), None),
        P("grp", None, None),
        P("grp", None, "node"),
        P("grp", None, "node"),
        P("grp", "node", None),
    )
    out_specs = P(("grp", "node"), None)
    return jax.shard_map(local, mesh=mesh, in_specs=in_specs, out_specs=out_specs, check_vma=False)
```

```python
import functools

import jax
import jax.numpy as jnp
from jax import lax
from jax.experimental import pallas as pl
from jax.experimental.pallas import tpu as pltpu
from jax.sharding import PartitionSpec as P

SPLIT = 8
C_DEV = 2
Z_STEP = 4
BLOCK = 128
META = 128
VMEM = 48 * 1024 * 1024
f32, bf16 = jnp.float32, jnp.bfloat16


def call(body, out_shape, cost, **kw):
    flops, moved = cost
    return pl.pallas_call(
        body,
        out_shape=out_shape,
        compiler_params=pltpu.CompilerParams(vmem_limit_bytes=VMEM),
        cost_estimate=pl.CostEstimate(
            flops=flops, bytes_accessed=moved, transcendentals=0
        ),
        **kw,
    )


def hbm(*arrays):
    return [pltpu.with_memory_space_constraint(a, pltpu.HBM) for a in arrays]


def swap(a, axis, members):
    return lax.all_to_all(a, axis, 0, 0, axis_index_groups=members, tiled=True)


def total(blocks):
    return functools.reduce(lambda p, q: p + q, [b.astype(f32) for b in blocks]).astype(bf16)


def pack_body(per_node, node_ref, grad_ref, ids_ref, slots_ref, gates_ref, out_ref, held):
    n_tok, n_pick = ids_ref.shape
    part = out_ref.shape[1] - META
    slots = slots_ref[...]
    slots = jnp.where(slots >= 0, slots - node_ref[0] * per_node, -1)
    held[...] = jnp.zeros_like(held)
    grad = grad_ref[...].astype(f32)
    for i in range(SPLIT):
        rows = slice(i * n_tok, (i + 1) * n_tok)
        held[rows, :part] = grad[:, i * part : (i + 1) * part]
        for j, field in enumerate((ids_ref[...], slots, gates_ref[...])):
            held[rows, part + j * n_pick : part + (j + 1) * n_pick] = field.astype(f32)
    out_ref[...] = held[...].astype(bf16)


def pack(node, grad, ids, slots, gates, per_node):
    n_tok, width = grad.shape
    shape = (SPLIT * n_tok, width // SPLIT + META)
    return call(
        functools.partial(pack_body, per_node),
        jax.ShapeDtypeStruct(shape, bf16),
        (0, 4 * n_tok * width),
        in_specs=[pl.BlockSpec(memory_space=pltpu.SMEM)]
        + [pl.BlockSpec(memory_space=pltpu.VMEM)] * 4,
        out_specs=pl.BlockSpec(memory_space=pltpu.VMEM),
        scratch_shapes=[pltpu.VMEM(shape, f32)],
    )(node, grad, ids, slots, gates)


def cut_body(gate_ref, up_ref, down_ref, out_ref, held, sem_in, sem_out):
    n = gate_ref.shape[0]
    part = out_ref.shape[2]
    come = [
        [
            pltpu.make_async_copy(
                ref.at[:, pl.ds(i * part, part)],
                held.at[i, pl.ds(j * n, n)],
                sem_in.at[i, j],
            )
            for j, ref in enumerate((gate_ref, up_ref, down_ref))
        ]
        for i in range(SPLIT)
    ]
    leave = [
        pltpu.make_async_copy(held.at[i], out_ref.at[i], sem_out.at[i])
        for i in range(SPLIT)
    ]
    for copies in come:
        for copy in copies:
            copy.start()
    for i in range(SPLIT):
        for copy in come[i]:
            copy.wait()
        leave[i].start()
    for copy in leave:
        copy.wait()


def cut_weights(gate, up, down):
    n_hid, width = gate.shape
    shape = (SPLIT, 3 * n_hid, width // SPLIT)
    return call(
        cut_body,
        pltpu.HBM(shape, bf16),
        (0, 12 * n_hid * width),
        in_specs=[pl.BlockSpec(memory_space=pl.ANY)] * 3,
        out_specs=pl.BlockSpec(memory_space=pl.ANY),
        scratch_shapes=[
            pltpu.VMEM(shape, bf16),
            pltpu.SemaphoreType.DMA((SPLIT, 3)),
            pltpu.SemaphoreType.DMA((SPLIT,)),
        ],
    )(*hbm(gate, up, down))


def coefficients(pre_gate, pre_up):
    squash = jax.nn.sigmoid(pre_gate)
    return pre_up * squash * (1.0 + pre_gate * (1.0 - squash)), pre_gate * squash


def early_body(run_ref, x_ref, gate_ref, up_ref, out_ref, held_x, held_w, sem_x, sem_w):
    n = gate_ref.shape[0]
    n_slot = x_ref.shape[0]
    rows = n_slot // sem_x.shape[0]

    @pl.when(run_ref[0] != 0)
    def _():
        weights = [
            pltpu.make_async_copy(ref, held_w.at[j], sem_w.at[j])
            for j, ref in enumerate((gate_ref, up_ref))
        ]
        inputs = [
            pltpu.make_async_copy(
                x_ref.at[pl.ds(i * rows, rows)],
                held_x.at[pl.ds(i * rows, rows)],
                sem_x.at[i],
            )
            for i in range(n_slot // rows)
        ]
        for copy in weights + inputs:
            copy.start()
        for copy in weights + inputs:
            copy.wait()
        for start in range(0, n_slot, BLOCK):
            pre_gate, pre_up = (
                lax.dot_general(
                    held_w[j],
                    held_x[start : start + BLOCK],
                    (((1,), (1,)), ((), ())),
                    preferred_element_type=f32,
                )
                for j in range(2)
            )
            for j, value in enumerate(coefficients(pre_gate, pre_up)):
                out_ref[j * n : (j + 1) * n, start : start + BLOCK] = value

    @pl.when(run_ref[0] == 0)
    def _():
        out_ref[...] = jnp.zeros_like(out_ref)


def early_forward(run, x, gate, up):
    n_slot, width = x.shape
    n_hid = gate.shape[0]
    return call(
        early_body,
        jax.ShapeDtypeStruct((2 * n_hid, n_slot), f32),
        (4 * n_hid * n_slot * width, 2 * (n_slot + 2 * n_hid) * width),
        in_specs=[pl.BlockSpec(memory_space=pltpu.SMEM)]
        + [pl.BlockSpec(memory_space=pl.ANY)] * 3,
        out_specs=pl.BlockSpec(memory_space=pltpu.VMEM),
        scratch_shapes=[
            pltpu.VMEM((n_slot, width), bf16),
            pltpu.VMEM((2, n_hid, width), bf16),
            pltpu.SemaphoreType.DMA((16,)),
            pltpu.SemaphoreType.DMA((2,)),
        ],
    )(run, *hbm(x, gate, up))


def late_body(run_ref, x_ref, gate_ref, up_ref, done_ref, out_ref):
    n = gate_ref.shape[0]

    @pl.when(run_ref[0] != 0)
    def _():
        both = jnp.concatenate([gate_ref[...], up_ref[...]], axis=0)
        pre = lax.dot_general(
            x_ref[...], both, (((1,), (1,)), ((), ())), preferred_element_type=f32
        ).T
        for j, value in enumerate(coefficients(pre[:n], pre[n:])):
            out_ref[j * n : (j + 1) * n] = value

    @pl.when(run_ref[0] == 0)
    def _():
        out_ref[...] = done_ref[...]


def late_forward(run, x, gate, up, done):
    n_slot, width = x.shape
    n_hid = gate.shape[0]
    half = n_slot // 2
    spec = pl.BlockSpec((n_hid, width), lambda i: (0, 0))
    out = pl.BlockSpec((2 * n_hid, half), lambda i: (0, i))
    return call(
        late_body,
        pltpu.HBM((2 * n_hid, n_slot), f32),
        (4 * n_hid * n_slot * width, 2 * (n_slot + 2 * n_hid) * width),
        grid=(2,),
        in_specs=[
            pl.BlockSpec(memory_space=pltpu.SMEM),
            pl.BlockSpec((half, width), lambda i: (i, 0)),
            spec,
            spec,
            out,
        ],
        out_specs=out,
    )(run, *hbm(x, gate, up), done)


def select_body(n_tok, per_node, n_pick, expert_ref, tok_ref, *refs):
    rows_ref, hot_ref = refs[-2:]
    part = rows_ref.shape[1]
    rout = tok_ref[:, part:].astype(f32)
    lane = lax.broadcasted_iota(jnp.int32, rout.shape, 1)
    row = lax.broadcasted_iota(jnp.int32, rout.shape, 0)
    slot = pltpu.roll(rout, META - n_pick, 1)
    gate = pltpu.roll(rout, META - 2 * n_pick, 1)
    hit = (lane < n_pick) & (rout == expert_ref[0].astype(f32)) & (slot >= 0)
    found = jnp.sum(jnp.where(hit, slot + 1.0, 0.0), axis=1, keepdims=True)
    scale = jnp.sum(jnp.where(hit, gate, 0.0), axis=1, keepdims=True) * (1.0 / 256.0)
    found = found.astype(jnp.int32) - 1
    node = (row // n_tok) % SPLIT
    one_hot = (found >= 0) & (node * per_node + found == lane)
    hot_ref[...] = jnp.where(one_hot, scale, 0.0).astype(bf16)
    pick = jnp.where(one_hot, 1.0, 0.0).T.astype(bf16)
    rows = jnp.dot(pick, tok_ref[:, :part], preferred_element_type=f32).astype(bf16)
    if len(refs) == 3:
        rows = rows + refs[0][...]
    for i in range(rows_ref.shape[0] // rows.shape[0]):
        rows_ref[i * rows.shape[0] : (i + 1) * rows.shape[0]] = rows


def select(expert, tokens, before, copies, n_tok, per_node, n_pick):
    n_all, wide = tokens.shape
    part = wide - META
    n_own = SPLIT * per_node
    return call(
        functools.partial(select_body, n_tok, per_node, n_pick),
        (
            (pltpu.HBM if before else jax.ShapeDtypeStruct)((copies * n_own, part), bf16),
            pltpu.HBM((n_all, n_own), bf16),
        ),
        (2 * n_all * n_own * part, 2 * n_all * wide),
        in_specs=[pl.BlockSpec(memory_space=pltpu.SMEM)]
        + [pl.BlockSpec(memory_space=pltpu.VMEM)] * (1 + len(before)),
        out_specs=[pl.BlockSpec(memory_space=pltpu.VMEM)] * 2,
    )(expert, tokens, *before)


def hidden_body(w_ref, rows_ref, out_ref):
    n, h, part = w_ref.shape
    got = lax.dot_general(
        w_ref[...].reshape(n * h, part),
        rows_ref[...],
        (((1,), (1,)), ((), ())),
        preferred_element_type=f32,
    )
    out_ref[...] = got.astype(bf16)


def hidden_part(weights, rows):
    n, h3, part = weights.shape
    h = h3 // 3
    n_slot = rows.shape[0]
    return call(
        hidden_body,
        pltpu.HBM((n * h, n_slot), bf16),
        (2 * n * h * n_slot * part, 2 * (n * h + n_slot) * part),
        grid=(1,),
        in_specs=[
            pl.BlockSpec((n, h, part), lambda i: (0, 2, 0)),
            pl.BlockSpec((n_slot, part), lambda i: (0, 0)),
        ],
        out_specs=pl.BlockSpec((n * h, n_slot), lambda i: (0, 0)),
    )(weights, rows)


def grads_body(parts_ref, coef_ref, out_ref, held, sem):
    n, h, _ = parts_ref.shape
    copy = pltpu.make_async_copy(coef_ref, held, sem)
    copy.start()
    total = jnp.sum(parts_ref[...].astype(f32), axis=0)
    copy.wait()
    grads = jnp.concatenate([total * held[:h], total * held[h:]], axis=0)
    grads = grads.T.astype(bf16)
    for i in range(n):
        out_ref[i] = grads


def grads_of(parts, coef):
    n, h, n_slot = parts.shape
    return call(
        grads_body,
        jax.ShapeDtypeStruct((n, n_slot, 2 * h), bf16),
        (2 * n * h * n_slot, 6 * n * h * n_slot),
        in_specs=[
            pl.BlockSpec(memory_space=pltpu.VMEM),
            pl.BlockSpec(memory_space=pl.ANY),
        ],
        out_specs=pl.BlockSpec(memory_space=pltpu.VMEM),
        scratch_shapes=[pltpu.VMEM((2 * h, n_slot), f32), pltpu.SemaphoreType.DMA],
    )(parts, *hbm(coef))


def slot_body(grads_ref, w_ref, out_ref):
    n, h, part = w_ref.shape
    grads = jnp.concatenate([grads_ref[i] for i in range(n)], axis=1)
    got = jnp.dot(grads, w_ref[...].reshape(n * h, part), preferred_element_type=f32)
    out_ref[...] = got.astype(bf16)


def slot_part(grads, weights):
    n, n_slot, h2 = grads.shape
    part = weights.shape[2]
    half = n_slot // 2
    return call(
        slot_body,
        jax.ShapeDtypeStruct((n_slot, part), bf16),
        (2 * n * h2 * n_slot * part, 2 * (n * h2 * (n_slot + part) + n_slot * part)),
        grid=(2,),
        in_specs=[
            pl.BlockSpec((n, half, h2), lambda i: (0, i, 0)),
            pl.BlockSpec((n, h2, part), lambda i: (0, 0, 0)),
        ],
        out_specs=pl.BlockSpec((half, part), lambda i: (i, 0)),
    )(grads, weights)


def back_body(order, hot_here_ref, hot_there_ref, parts_ref, here_ref, there_ref):
    own = jnp.sum(parts_ref[...].astype(f32), axis=0).astype(bf16)
    rows = here_ref.shape[0] // len(order)
    for hot_ref, out_ref in ((hot_there_ref, there_ref), (hot_here_ref, here_ref)):
        got = jnp.dot(hot_ref[...], own, preferred_element_type=f32).astype(bf16)
        for i, z in enumerate(order):
            out_ref[i * rows : (i + 1) * rows] = got[z * rows : (z + 1) * rows]


def back_rows(order, hot_here, hot_there, parts):
    half, n_own = hot_here.shape
    part = parts.shape[2]
    return call(
        functools.partial(back_body, order),
        (jax.ShapeDtypeStruct((half, part), bf16),) * 2,
        (4 * half * n_own * part, 4 * half * part + 2 * parts.size),
    )(hot_here, hot_there, parts)


def unpack_body(parts_ref, out_ref):
    n_tok = out_ref.shape[0]
    added = jnp.sum(parts_ref[...].astype(f32), axis=0)
    pieces = [added[i * n_tok : (i + 1) * n_tok] for i in range(SPLIT)]
    out_ref[...] = jnp.concatenate(pieces, axis=1).astype(bf16)


def unpack(parts, n_tok):
    return call(
        unpack_body,
        jax.ShapeDtypeStruct((n_tok, SPLIT * parts.shape[2]), bf16),
        (parts.size, 2 * parts.size),
    )(parts)


def local(out_grad, expert_ids, slot_ids, gate_q, saved_x, w_gate, w_up, w_down):
    n_grp, n_node = lax.axis_size("grp"), lax.axis_size("node")
    my_expert, my_node = lax.axis_index("grp"), lax.axis_index("node")
    n_rest, n_z = n_node // SPLIT, n_grp // C_DEV
    block = [[h * SPLIT + d for d in range(SPLIT)] for h in range(n_rest)]
    along_z = [
        [z * C_DEV + (c + z // 2) % C_DEV for z in range(n_z)] for c in range(C_DEV)
    ]
    order = [z for first in range(Z_STEP) for z in range(first, n_z, Z_STEP)]
    other = [(z * C_DEV + c, z * C_DEV + 1 - c) for z in range(n_z) for c in range(C_DEV)]
    n_tok, width = out_grad.shape
    part = width // SPLIT
    n_slot = saved_x.shape[1]
    per_node = n_slot // n_node
    n_hid = w_down.shape[1]
    n_pick = expert_ids.shape[1]
    n_own = SPLIT * per_node
    gate, up, down = w_gate[0].T, w_up[0].T, w_down[0]

    payload = pack(my_node.astype(jnp.int32).reshape(1), out_grad, expert_ids, slot_ids, gate_q, per_node)

    weights = cut_weights(gate, up, down)
    payload, weights = lax.optimization_barrier((payload, weights))
    weights = swap(weights, "node", block)

    here = lax.all_gather(payload, "grp", axis=0, axis_index_groups=along_z, tiled=True)
    there = lax.ppermute(here, "grp", other)
    expert = my_expert.astype(jnp.int32).reshape(1)
    rows, hot_here = select(expert, here, (), 1, n_tok, per_node, n_pick)
    rows, hot_there = select(expert, there, (rows,), n_rest, n_tok, per_node, n_pick)
    late = (my_expert % C_DEV).astype(jnp.int32).reshape(1)
    gate, rows = lax.optimization_barrier((gate, rows))
    coef = early_forward(late, saved_x[0], gate, up)
    rows, weights, coef = lax.optimization_barrier((rows, weights, coef))
    rows = lax.all_to_all(rows, "node", 0, 0, tiled=True)

    gate, rows = lax.optimization_barrier((gate, rows))
    hidden = swap(hidden_part(weights, rows), "node", block)
    hidden = hidden.reshape(SPLIT, n_hid, n_slot)
    coef = late_forward(1 - late, saved_x[0], gate, up, coef)
    grads = swap(grads_of(hidden, coef), "node", block)
    parts = lax.all_to_all(slot_part(grads, weights), "node", 0, 0, tiled=True)

    here, there = back_rows(order, hot_here, hot_there, parts.reshape(n_rest, n_own, part))
    back = total([here, lax.ppermute(there, "grp", other)])
    back = swap(back, "grp", [[ring[z] for z in order] for ring in along_z]).reshape(n_z, SPLIT * n_tok, part)
    return unpack(back, n_tok)


def solution(mesh):
    in_specs = (
        P(("grp", "node"), None),
        P(("grp", "node"), None),
        P(("grp", "node"), None),
        P(("grp", "node"), None),
        P("grp", None, None),
        P("grp", None, "node"),
        P("grp", None, "node"),
        P("grp", "node", None),
    )
    out_specs = P(("grp", "node"), None)
    return jax.shard_map(local, mesh=mesh, in_specs=in_specs, out_specs=out_specs, check_vma=False)
```

```python
import functools

import jax
import jax.numpy as jnp
from jax import lax
from jax.experimental import pallas as pl
from jax.experimental.pallas import tpu as pltpu
from jax.sharding import PartitionSpec as P

SPLIT = 8
C_DEV = 2
RING = 2
BLOCK = 128
META = 128
VMEM = 48 * 1024 * 1024
f32, bf16 = jnp.float32, jnp.bfloat16


def call(body, out_shape, cost, **kw):
    flops, moved = cost
    return pl.pallas_call(
        body,
        out_shape=out_shape,
        compiler_params=pltpu.CompilerParams(vmem_limit_bytes=VMEM),
        cost_estimate=pl.CostEstimate(
            flops=flops, bytes_accessed=moved, transcendentals=0
        ),
        **kw,
    )


def hbm(*arrays):
    return [pltpu.with_memory_space_constraint(a, pltpu.HBM) for a in arrays]


def swap(a, axis, members):
    return lax.all_to_all(a, axis, 0, 0, axis_index_groups=members, tiled=True)


def total(blocks):
    return functools.reduce(lambda p, q: p + q, [b.astype(f32) for b in blocks]).astype(bf16)


def pack_body(per_node, node_ref, grad_ref, ids_ref, slots_ref, gates_ref, out_ref, held):
    n_tok, n_pick = ids_ref.shape
    part = out_ref.shape[1] - META
    slots = slots_ref[...]
    slots = jnp.where(slots >= 0, slots - node_ref[0] * per_node, -1)
    held[...] = jnp.zeros_like(held)
    grad = grad_ref[...].astype(f32)
    for i in range(SPLIT):
        rows = slice(i * n_tok, (i + 1) * n_tok)
        held[rows, :part] = grad[:, i * part : (i + 1) * part]
        for j, field in enumerate((ids_ref[...], slots, gates_ref[...])):
            held[rows, part + j * n_pick : part + (j + 1) * n_pick] = field.astype(f32)
    out_ref[...] = held[...].astype(bf16)


def pack(node, grad, ids, slots, gates, per_node):
    n_tok, width = grad.shape
    shape = (SPLIT * n_tok, width // SPLIT + META)
    return call(
        functools.partial(pack_body, per_node),
        jax.ShapeDtypeStruct(shape, bf16),
        (0, 4 * n_tok * width),
        in_specs=[pl.BlockSpec(memory_space=pltpu.SMEM)]
        + [pl.BlockSpec(memory_space=pltpu.VMEM)] * 4,
        out_specs=pl.BlockSpec(memory_space=pltpu.VMEM),
        scratch_shapes=[pltpu.VMEM(shape, f32)],
    )(node, grad, ids, slots, gates)


def cut_body(gate_ref, up_ref, down_ref, out_ref, held, sem_in, sem_out):
    n = gate_ref.shape[0]
    part = out_ref.shape[2]
    come = [
        [
            pltpu.make_async_copy(
                ref.at[:, pl.ds(i * part, part)],
                held.at[i, pl.ds(j * n, n)],
                sem_in.at[i, j],
            )
            for j, ref in enumerate((gate_ref, up_ref, down_ref))
        ]
        for i in range(SPLIT)
    ]
    leave = [
        pltpu.make_async_copy(held.at[i], out_ref.at[i], sem_out.at[i])
        for i in range(SPLIT)
    ]
    for copies in come:
        for copy in copies:
            copy.start()
    for i in range(SPLIT):
        for copy in come[i]:
            copy.wait()
        leave[i].start()
    for copy in leave:
        copy.wait()


def cut_weights(gate, up, down):
    n_hid, width = gate.shape
    shape = (SPLIT, 3 * n_hid, width // SPLIT)
    return call(
        cut_body,
        pltpu.HBM(shape, bf16),
        (0, 12 * n_hid * width),
        in_specs=[pl.BlockSpec(memory_space=pl.ANY)] * 3,
        out_specs=pl.BlockSpec(memory_space=pl.ANY),
        scratch_shapes=[
            pltpu.VMEM(shape, bf16),
            pltpu.SemaphoreType.DMA((SPLIT, 3)),
            pltpu.SemaphoreType.DMA((SPLIT,)),
        ],
    )(*hbm(gate, up, down))


def coefficients(pre_gate, pre_up):
    squash = jax.nn.sigmoid(pre_gate)
    return pre_up * squash * (1.0 + pre_gate * (1.0 - squash)), pre_gate * squash


def early_body(run_ref, x_ref, gate_ref, up_ref, out_ref, held_x, held_w, sem_x, sem_w):
    n = gate_ref.shape[0]
    n_slot = x_ref.shape[0]
    rows = n_slot // sem_x.shape[0]

    @pl.when(run_ref[0] != 0)
    def _():
        weights = [
            pltpu.make_async_copy(ref, held_w.at[j], sem_w.at[j])
            for j, ref in enumerate((gate_ref, up_ref))
        ]
        inputs = [
            pltpu.make_async_copy(
                x_ref.at[pl.ds(i * rows, rows)],
                held_x.at[pl.ds(i * rows, rows)],
                sem_x.at[i],
            )
            for i in range(n_slot // rows)
        ]
        for copy in weights + inputs:
            copy.start()
        for copy in weights:
            copy.wait()
        for start in range(0, n_slot, BLOCK):
            for i in range(start // rows, (start + BLOCK) // rows):
                inputs[i].wait()
            pre_gate, pre_up = (
                lax.dot_general(
                    held_w[j],
                    held_x[start : start + BLOCK],
                    (((1,), (1,)), ((), ())),
                    preferred_element_type=f32,
                )
                for j in range(2)
            )
            for j, value in enumerate(coefficients(pre_gate, pre_up)):
                out_ref[j * n : (j + 1) * n, start : start + BLOCK] = value

    @pl.when(run_ref[0] == 0)
    def _():
        out_ref[...] = jnp.zeros_like(out_ref)


def early_forward(run, x, gate, up):
    n_slot, width = x.shape
    n_hid = gate.shape[0]
    return call(
        early_body,
        jax.ShapeDtypeStruct((2 * n_hid, n_slot), f32),
        (4 * n_hid * n_slot * width, 2 * (n_slot + 2 * n_hid) * width),
        in_specs=[pl.BlockSpec(memory_space=pltpu.SMEM)]
        + [pl.BlockSpec(memory_space=pl.ANY)] * 3,
        out_specs=pl.BlockSpec(memory_space=pltpu.VMEM),
        scratch_shapes=[
            pltpu.VMEM((n_slot, width), bf16),
            pltpu.VMEM((2, n_hid, width), bf16),
            pltpu.SemaphoreType.DMA((16,)),
            pltpu.SemaphoreType.DMA((2,)),
        ],
    )(run, *hbm(x, gate, up))


def late_body(run_ref, x_ref, gate_ref, up_ref, done_ref, out_ref):
    n = gate_ref.shape[0]

    @pl.when(run_ref[0] != 0)
    def _():
        both = jnp.concatenate([gate_ref[...], up_ref[...]], axis=0)
        pre = lax.dot_general(
            x_ref[...], both, (((1,), (1,)), ((), ())), preferred_element_type=f32
        ).T
        for j, value in enumerate(coefficients(pre[:n], pre[n:])):
            out_ref[j * n : (j + 1) * n] = value

    @pl.when(run_ref[0] == 0)
    def _():
        out_ref[...] = done_ref[...]


def late_forward(run, x, gate, up, done):
    n_slot, width = x.shape
    n_hid = gate.shape[0]
    half = n_slot // 2
    spec = pl.BlockSpec((n_hid, width), lambda i: (0, 0))
    out = pl.BlockSpec((2 * n_hid, half), lambda i: (0, i))
    return call(
        late_body,
        pltpu.HBM((2 * n_hid, n_slot), f32),
        (4 * n_hid * n_slot * width, 2 * (n_slot + 2 * n_hid) * width),
        grid=(2,),
        in_specs=[
            pl.BlockSpec(memory_space=pltpu.SMEM),
            pl.BlockSpec((half, width), lambda i: (i, 0)),
            spec,
            spec,
            out,
        ],
        out_specs=out,
    )(run, *hbm(x, gate, up), done)


def select_body(n_tok, per_node, n_pick, expert_ref, tok_ref, *refs):
    rows_ref, hot_ref = refs[-2:]
    part = rows_ref.shape[1]
    rout = tok_ref[:, part:].astype(f32)
    lane = lax.broadcasted_iota(jnp.int32, rout.shape, 1)
    row = lax.broadcasted_iota(jnp.int32, rout.shape, 0)
    slot = pltpu.roll(rout, META - n_pick, 1)
    gate = pltpu.roll(rout, META - 2 * n_pick, 1)
    hit = (lane < n_pick) & (rout == expert_ref[0].astype(f32)) & (slot >= 0)
    found = jnp.sum(jnp.where(hit, slot + 1.0, 0.0), axis=1, keepdims=True)
    scale = jnp.sum(jnp.where(hit, gate, 0.0), axis=1, keepdims=True) * (1.0 / 256.0)
    found = found.astype(jnp.int32) - 1
    node = (row // n_tok) % SPLIT
    one_hot = (found >= 0) & (node * per_node + found == lane)
    hot_ref[...] = jnp.where(one_hot, scale, 0.0).astype(bf16)
    pick = jnp.where(one_hot, 1.0, 0.0).T.astype(bf16)
    rows = jnp.dot(pick, tok_ref[:, :part], preferred_element_type=f32).astype(bf16)
    if len(refs) == 3:
        rows = rows + refs[0][...]
    for i in range(rows_ref.shape[0] // rows.shape[0]):
        rows_ref[i * rows.shape[0] : (i + 1) * rows.shape[0]] = rows


def select(expert, tokens, before, copies, n_tok, per_node, n_pick):
    n_all, wide = tokens.shape
    part = wide - META
    n_own = SPLIT * per_node
    return call(
        functools.partial(select_body, n_tok, per_node, n_pick),
        (
            (pltpu.HBM if before else jax.ShapeDtypeStruct)((copies * n_own, part), bf16),
            pltpu.HBM((n_all, n_own), bf16),
        ),
        (2 * n_all * n_own * part, 2 * n_all * wide),
        in_specs=[pl.BlockSpec(memory_space=pltpu.SMEM)]
        + [pl.BlockSpec(memory_space=pltpu.VMEM)] * (1 + len(before)),
        out_specs=[pl.BlockSpec(memory_space=pltpu.VMEM)] * 2,
    )(expert, tokens, *before)


def hidden_body(w_ref, rows_ref, out_ref):
    n, h, part = w_ref.shape
    got = lax.dot_general(
        w_ref[...].reshape(n * h, part),
        rows_ref[...],
        (((1,), (1,)), ((), ())),
        preferred_element_type=f32,
    )
    out_ref[...] = got.astype(bf16)


def hidden_part(weights, rows):
    n, h3, part = weights.shape
    h = h3 // 3
    n_slot = rows.shape[0]
    return call(
        hidden_body,
        pltpu.HBM((n * h, n_slot), bf16),
        (2 * n * h * n_slot * part, 2 * (n * h + n_slot) * part),
        grid=(1,),
        in_specs=[
            pl.BlockSpec((n, h, part), lambda i: (0, 2, 0)),
            pl.BlockSpec((n_slot, part), lambda i: (0, 0)),
        ],
        out_specs=pl.BlockSpec((n * h, n_slot), lambda i: (0, 0)),
    )(weights, rows)


def grads_body(parts_ref, coef_ref, out_ref):
    n, h, _ = parts_ref.shape
    total = jnp.sum(parts_ref[...].astype(f32), axis=0)
    grads = jnp.concatenate([total * coef_ref[:h], total * coef_ref[h:]], axis=0)
    grads = grads.T.astype(bf16)
    for i in range(n):
        out_ref[i] = grads


def grads_of(parts, coef):
    n, h, n_slot = parts.shape
    return call(
        grads_body,
        jax.ShapeDtypeStruct((n, n_slot, 2 * h), bf16),
        (2 * n * h * n_slot, 6 * n * h * n_slot),
    )(parts, *hbm(coef))


def slot_body(grads_ref, w_ref, out_ref):
    n, h, part = w_ref.shape
    grads = jnp.concatenate([grads_ref[i] for i in range(n)], axis=1)
    got = jnp.dot(grads, w_ref[...].reshape(n * h, part), preferred_element_type=f32)
    out_ref[...] = got.astype(bf16)


def slot_part(grads, weights):
    n, n_slot, h2 = grads.shape
    part = weights.shape[2]
    half = n_slot // 2
    return call(
        slot_body,
        jax.ShapeDtypeStruct((n_slot, part), bf16),
        (2 * n * h2 * n_slot * part, 2 * (n * h2 * (n_slot + part) + n_slot * part)),
        grid=(2,),
        in_specs=[
            pl.BlockSpec((n, half, h2), lambda i: (0, i, 0)),
            pl.BlockSpec((n, h2, part), lambda i: (0, 0, 0)),
        ],
        out_specs=pl.BlockSpec((half, part), lambda i: (i, 0)),
    )(grads, weights)


def back_body(order, flip_ref, hot_here_ref, hot_there_ref, parts_ref, here_ref, there_ref):
    own = jnp.sum(parts_ref[...].astype(f32), axis=0).astype(bf16)
    rows = here_ref.shape[0] // len(order)
    z = lax.broadcasted_iota(jnp.int32, hot_here_ref.shape, 0) // rows
    same = (z // RING) % C_DEV == flip_ref[0]
    here, there = hot_here_ref[...].astype(f32), hot_there_ref[...].astype(f32)
    for hot, out_ref in (
        (jnp.where(same, there, here), there_ref),
        (jnp.where(same, here, there), here_ref),
    ):
        got = jnp.dot(hot.astype(bf16), own, preferred_element_type=f32).astype(bf16)
        for i, z in enumerate(order):
            out_ref[i * rows : (i + 1) * rows] = got[z * rows : (z + 1) * rows]


def back_rows(order, flip, hot_here, hot_there, parts):
    half, n_own = hot_here.shape
    part = parts.shape[2]
    return call(
        functools.partial(back_body, order),
        (jax.ShapeDtypeStruct((half, part), bf16),) * 2,
        (4 * half * n_own * part, 4 * half * part + 2 * parts.size),
        in_specs=[pl.BlockSpec(memory_space=pltpu.SMEM)]
        + [pl.BlockSpec(memory_space=pltpu.VMEM)] * 3,
        out_specs=[pl.BlockSpec(memory_space=pltpu.VMEM)] * 2,
    )(flip, hot_here, hot_there, parts)


def unpack_body(parts_ref, out_ref):
    n_tok = out_ref.shape[0]
    added = jnp.sum(parts_ref[...].astype(f32), axis=0)
    pieces = [added[i * n_tok : (i + 1) * n_tok] for i in range(SPLIT)]
    out_ref[...] = jnp.concatenate(pieces, axis=1).astype(bf16)


def unpack(parts, n_tok):
    return call(
        unpack_body,
        jax.ShapeDtypeStruct((n_tok, SPLIT * parts.shape[2]), bf16),
        (parts.size, 2 * parts.size),
    )(parts)


def local(out_grad, expert_ids, slot_ids, gate_q, saved_x, w_gate, w_up, w_down):
    n_grp, n_node = lax.axis_size("grp"), lax.axis_size("node")
    my_expert, my_node = lax.axis_index("grp"), lax.axis_index("node")
    n_rest, n_z = n_node // SPLIT, n_grp // C_DEV
    block = [[h * SPLIT + d for d in range(SPLIT)] for h in range(n_rest)]
    along_z = [
        [z * C_DEV + (c + z // RING) % C_DEV for z in range(n_z)] for c in range(C_DEV)
    ]
    order = list(range(0, n_z, 2)) + list(range(1, n_z, 2))
    other = [(z * C_DEV + c, z * C_DEV + 1 - c) for z in range(n_z) for c in range(C_DEV)]
    n_tok, width = out_grad.shape
    part = width // SPLIT
    n_slot = saved_x.shape[1]
    per_node = n_slot // n_node
    n_hid = w_down.shape[1]
    n_pick = expert_ids.shape[1]
    n_own = SPLIT * per_node
    gate, up, down = w_gate[0].T, w_up[0].T, w_down[0]

    payload = pack(my_node.astype(jnp.int32).reshape(1), out_grad, expert_ids, slot_ids, gate_q, per_node)

    weights = cut_weights(gate, up, down)
    payload, weights = lax.optimization_barrier((payload, weights))
    weights = swap(weights, "node", block)

    here = lax.all_gather(payload, "grp", axis=0, axis_index_groups=along_z, tiled=True)
    there = lax.ppermute(here, "grp", other)
    expert = my_expert.astype(jnp.int32).reshape(1)
    rows, hot_here = select(expert, here, (), 1, n_tok, per_node, n_pick)
    rows, hot_there = select(expert, there, (rows,), n_rest, n_tok, per_node, n_pick)
    late = (my_expert % C_DEV).astype(jnp.int32).reshape(1)
    gate, rows = lax.optimization_barrier((gate, rows))
    coef = early_forward(late, saved_x[0], gate, up)
    rows, weights, coef = lax.optimization_barrier((rows, weights, coef))
    rows = lax.all_to_all(rows, "node", 0, 0, tiled=True)

    gate, rows = lax.optimization_barrier((gate, rows))
    hidden = swap(hidden_part(weights, rows), "node", block)
    hidden = hidden.reshape(SPLIT, n_hid, n_slot)
    coef = late_forward(1 - late, saved_x[0], gate, up, coef)
    grads = swap(grads_of(hidden, coef), "node", block)
    parts = lax.all_to_all(slot_part(grads, weights), "node", 0, 0, tiled=True)

    flip = (my_expert // C_DEV // RING % C_DEV).astype(jnp.int32).reshape(1)
    here, there = back_rows(order, flip, hot_here, hot_there, parts.reshape(n_rest, n_own, part))
    back = total([here, lax.ppermute(there, "grp", other)])
    back = swap(back, "grp", [[z * C_DEV + c for z in order] for c in range(C_DEV)]).reshape(n_z, SPLIT * n_tok, part)
    return unpack(back, n_tok)


def solution(mesh):
    in_specs = (
        P(("grp", "node"), None),
        P(("grp", "node"), None),
        P(("grp", "node"), None),
        P(("grp", "node"), None),
        P("grp", None, None),
        P("grp", None, "node"),
        P("grp", None, "node"),
        P("grp", "node", None),
    )
    out_specs = P(("grp", "node"), None)
    return jax.shard_map(local, mesh=mesh, in_specs=in_specs, out_specs=out_specs, check_vma=False)
```

```python
import functools

import jax
import jax.numpy as jnp
from jax import lax
from jax.experimental import pallas as pl
from jax.experimental.pallas import tpu as pltpu
from jax.sharding import PartitionSpec as P

SPLIT = 8
C_DEV = 2
BLOCK = 128
META = 128
VMEM = 48 * 1024 * 1024
f32, bf16 = jnp.float32, jnp.bfloat16


def call(body, out_shape, cost, **kw):
    flops, moved = cost
    return pl.pallas_call(
        body,
        out_shape=out_shape,
        compiler_params=pltpu.CompilerParams(vmem_limit_bytes=VMEM),
        cost_estimate=pl.CostEstimate(
            flops=flops, bytes_accessed=moved, transcendentals=0
        ),
        **kw,
    )


def hbm(*arrays):
    return [pltpu.with_memory_space_constraint(a, pltpu.HBM) for a in arrays]


def swap(a, axis, members):
    return lax.all_to_all(a, axis, 0, 0, axis_index_groups=members, tiled=True)


def total(blocks):
    return functools.reduce(lambda p, q: p + q, [b.astype(f32) for b in blocks]).astype(bf16)


def pack_body(per_node, node_ref, grad_ref, ids_ref, slots_ref, gates_ref, out_ref, held):
    n_tok, n_pick = ids_ref.shape
    part = out_ref.shape[1] - META
    slots = slots_ref[...]
    slots = jnp.where(slots >= 0, slots - node_ref[0] * per_node, -1)
    held[...] = jnp.zeros_like(held)
    grad = grad_ref[...].astype(f32)
    for i in range(SPLIT):
        rows = slice(i * n_tok, (i + 1) * n_tok)
        held[rows, :part] = grad[:, i * part : (i + 1) * part]
        for j, field in enumerate((ids_ref[...], slots, gates_ref[...])):
            held[rows, part + j * n_pick : part + (j + 1) * n_pick] = field.astype(f32)
    out_ref[...] = held[...].astype(bf16)


def pack(node, grad, ids, slots, gates, per_node):
    n_tok, width = grad.shape
    shape = (SPLIT * n_tok, width // SPLIT + META)
    return call(
        functools.partial(pack_body, per_node),
        jax.ShapeDtypeStruct(shape, bf16),
        (0, 4 * n_tok * width),
        in_specs=[pl.BlockSpec(memory_space=pltpu.SMEM)]
        + [pl.BlockSpec(memory_space=pltpu.VMEM)] * 4,
        out_specs=pl.BlockSpec(memory_space=pltpu.VMEM),
        scratch_shapes=[pltpu.VMEM(shape, f32)],
    )(node, grad, ids, slots, gates)


def cut_body(gate_ref, up_ref, down_ref, out_ref, held, sem_in, sem_out):
    n = gate_ref.shape[0]
    part = out_ref.shape[2]
    come = [
        [
            pltpu.make_async_copy(
                ref.at[:, pl.ds(i * part, part)],
                held.at[i, pl.ds(j * n, n)],
                sem_in.at[i, j],
            )
            for j, ref in enumerate((gate_ref, up_ref, down_ref))
        ]
        for i in range(SPLIT)
    ]
    leave = [
        pltpu.make_async_copy(held.at[i], out_ref.at[i], sem_out.at[i])
        for i in range(SPLIT)
    ]
    for copies in come:
        for copy in copies:
            copy.start()
    for i in range(SPLIT):
        for copy in come[i]:
            copy.wait()
        leave[i].start()
    for copy in leave:
        copy.wait()


def cut_weights(gate, up, down):
    n_hid, width = gate.shape
    shape = (SPLIT, 3 * n_hid, width // SPLIT)
    return call(
        cut_body,
        pltpu.HBM(shape, bf16),
        (0, 12 * n_hid * width),
        in_specs=[pl.BlockSpec(memory_space=pl.ANY)] * 3,
        out_specs=pl.BlockSpec(memory_space=pl.ANY),
        scratch_shapes=[
            pltpu.VMEM(shape, bf16),
            pltpu.SemaphoreType.DMA((SPLIT, 3)),
            pltpu.SemaphoreType.DMA((SPLIT,)),
        ],
    )(*hbm(gate, up, down))


def coefficients(pre_gate, pre_up):
    squash = jax.nn.sigmoid(pre_gate)
    return pre_up * squash * (1.0 + pre_gate * (1.0 - squash)), pre_gate * squash


def early_body(run_ref, x_ref, gate_ref, up_ref, out_ref, held_x, held_w, sem_x, sem_w):
    n = gate_ref.shape[0]
    n_slot = x_ref.shape[0]
    rows = n_slot // sem_x.shape[0]

    @pl.when(run_ref[0] != 0)
    def _():
        weights = [
            pltpu.make_async_copy(ref, held_w.at[j], sem_w.at[j])
            for j, ref in enumerate((gate_ref, up_ref))
        ]
        inputs = [
            pltpu.make_async_copy(
                x_ref.at[pl.ds(i * rows, rows)],
                held_x.at[pl.ds(i * rows, rows)],
                sem_x.at[i],
            )
            for i in range(n_slot // rows)
        ]
        for copy in weights + inputs:
            copy.start()
        for copy in weights:
            copy.wait()
        for start in range(0, n_slot, BLOCK):
            for i in range(start // rows, (start + BLOCK) // rows):
                inputs[i].wait()
            pre_gate, pre_up = (
                lax.dot_general(
                    held_w[j],
                    held_x[start : start + BLOCK],
                    (((1,), (1,)), ((), ())),
                    preferred_element_type=f32,
                )
                for j in range(2)
            )
            for j, value in enumerate(coefficients(pre_gate, pre_up)):
                out_ref[j * n : (j + 1) * n, start : start + BLOCK] = value.astype(bf16)

    @pl.when(run_ref[0] == 0)
    def _():
        out_ref[...] = jnp.zeros_like(out_ref)


def early_forward(run, x, gate, up):
    n_slot, width = x.shape
    n_hid = gate.shape[0]
    return call(
        early_body,
        jax.ShapeDtypeStruct((2 * n_hid, n_slot), bf16),
        (4 * n_hid * n_slot * width, 2 * (n_slot + 2 * n_hid) * width),
        in_specs=[pl.BlockSpec(memory_space=pltpu.SMEM)]
        + [pl.BlockSpec(memory_space=pl.ANY)] * 3,
        out_specs=pl.BlockSpec(memory_space=pltpu.VMEM),
        scratch_shapes=[
            pltpu.VMEM((n_slot, width), bf16),
            pltpu.VMEM((2, n_hid, width), bf16),
            pltpu.SemaphoreType.DMA((16,)),
            pltpu.SemaphoreType.DMA((2,)),
        ],
    )(run, *hbm(x, gate, up))


def late_body(run_ref, x_ref, gate_ref, up_ref, done_ref, out_ref):
    n = gate_ref.shape[0]

    @pl.when(run_ref[0] != 0)
    def _():
        both = jnp.concatenate([gate_ref[...], up_ref[...]], axis=0)
        pre = lax.dot_general(
            x_ref[...], both, (((1,), (1,)), ((), ())), preferred_element_type=f32
        ).T
        for j, value in enumerate(coefficients(pre[:n], pre[n:])):
            out_ref[j * n : (j + 1) * n] = value.astype(bf16)

    @pl.when(run_ref[0] == 0)
    def _():
        out_ref[...] = done_ref[...]


def late_forward(run, x, gate, up, done):
    n_slot, width = x.shape
    n_hid = gate.shape[0]
    half = n_slot // 2
    spec = pl.BlockSpec((n_hid, width), lambda i: (0, 0))
    out = pl.BlockSpec((2 * n_hid, half), lambda i: (0, i))
    return call(
        late_body,
        pltpu.HBM((2 * n_hid, n_slot), bf16),
        (4 * n_hid * n_slot * width, 2 * (n_slot + 2 * n_hid) * width),
        grid=(2,),
        in_specs=[
            pl.BlockSpec(memory_space=pltpu.SMEM),
            pl.BlockSpec((half, width), lambda i: (i, 0)),
            spec,
            spec,
            out,
        ],
        out_specs=out,
    )(run, *hbm(x, gate, up), done)


def select_body(n_tok, per_node, n_pick, expert_ref, tok_ref, *refs):
    rows_ref, hot_ref = refs[-2:]
    part = rows_ref.shape[1]
    rout = tok_ref[:, part:].astype(f32)
    lane = lax.broadcasted_iota(jnp.int32, rout.shape, 1)
    row = lax.broadcasted_iota(jnp.int32, rout.shape, 0)
    slot = pltpu.roll(rout, META - n_pick, 1)
    gate = pltpu.roll(rout, META - 2 * n_pick, 1)
    hit = (lane < n_pick) & (rout == expert_ref[0].astype(f32)) & (slot >= 0)
    found = jnp.sum(jnp.where(hit, slot + 1.0, 0.0), axis=1, keepdims=True)
    scale = jnp.sum(jnp.where(hit, gate, 0.0), axis=1, keepdims=True) * (1.0 / 256.0)
    found = found.astype(jnp.int32) - 1
    node = (row // n_tok) % SPLIT
    one_hot = (found >= 0) & (node * per_node + found == lane)
    hot_ref[...] = jnp.where(one_hot, scale, 0.0).astype(bf16)
    pick = jnp.where(one_hot, 1.0, 0.0).T.astype(bf16)
    rows = jnp.dot(pick, tok_ref[:, :part], preferred_element_type=f32).astype(bf16)
    if len(refs) == 3:
        rows = rows + refs[0][...]
    for i in range(rows_ref.shape[0] // rows.shape[0]):
        rows_ref[i * rows.shape[0] : (i + 1) * rows.shape[0]] = rows


def select(expert, tokens, before, copies, n_tok, per_node, n_pick):
    n_all, wide = tokens.shape
    part = wide - META
    n_own = SPLIT * per_node
    return call(
        functools.partial(select_body, n_tok, per_node, n_pick),
        (
            (pltpu.HBM if before else jax.ShapeDtypeStruct)((copies * n_own, part), bf16),
            pltpu.HBM((n_all, n_own), bf16),
        ),
        (2 * n_all * n_own * part, 2 * n_all * wide),
        in_specs=[pl.BlockSpec(memory_space=pltpu.SMEM)]
        + [pl.BlockSpec(memory_space=pltpu.VMEM)] * (1 + len(before)),
        out_specs=[pl.BlockSpec(memory_space=pltpu.VMEM)] * 2,
    )(expert, tokens, *before)


def hidden_body(w_ref, rows_ref, out_ref):
    n, h, part = w_ref.shape
    got = lax.dot_general(
        w_ref[...].reshape(n * h, part),
        rows_ref[...],
        (((1,), (1,)), ((), ())),
        preferred_element_type=f32,
    )
    out_ref[...] = got.astype(bf16)


def hidden_part(weights, rows):
    n, h3, part = weights.shape
    h = h3 // 3
    n_slot = rows.shape[0]
    return call(
        hidden_body,
        pltpu.HBM((n * h, n_slot), bf16),
        (2 * n * h * n_slot * part, 2 * (n * h + n_slot) * part),
        grid=(1,),
        in_specs=[
            pl.BlockSpec((n, h, part), lambda i: (0, 2, 0)),
            pl.BlockSpec((n_slot, part), lambda i: (0, 0)),
        ],
        out_specs=pl.BlockSpec((n * h, n_slot), lambda i: (0, 0)),
    )(weights, rows)


def grads_body(parts_ref, coef_ref, out_ref):
    n, h, _ = parts_ref.shape
    total = jnp.sum(parts_ref[...].astype(f32), axis=0)
    coef = coef_ref[...].astype(f32)
    grads = jnp.concatenate([total * coef[:h], total * coef[h:]], axis=0)
    grads = grads.T.astype(bf16)
    for i in range(n):
        out_ref[i] = grads


def grads_of(parts, coef):
    n, h, n_slot = parts.shape
    return call(
        grads_body,
        jax.ShapeDtypeStruct((n, n_slot, 2 * h), bf16),
        (2 * n * h * n_slot, 6 * n * h * n_slot),
    )(parts, *hbm(coef))


def slot_body(grads_ref, w_ref, out_ref):
    n, h, part = w_ref.shape
    grads = jnp.concatenate([grads_ref[i] for i in range(n)], axis=1)
    got = jnp.dot(grads, w_ref[...].reshape(n * h, part), preferred_element_type=f32)
    out_ref[...] = got.astype(bf16)


def slot_part(grads, weights):
    n, n_slot, h2 = grads.shape
    part = weights.shape[2]
    half = n_slot // 2
    return call(
        slot_body,
        jax.ShapeDtypeStruct((n_slot, part), bf16),
        (2 * n * h2 * n_slot * part, 2 * (n * h2 * (n_slot + part) + n_slot * part)),
        grid=(2,),
        in_specs=[
            pl.BlockSpec((n, half, h2), lambda i: (0, i, 0)),
            pl.BlockSpec((n, h2, part), lambda i: (0, 0, 0)),
        ],
        out_specs=pl.BlockSpec((half, part), lambda i: (i, 0)),
    )(grads, weights)


def back_body(hot_here_ref, hot_there_ref, parts_ref, here_ref, there_ref):
    own = jnp.sum(parts_ref[...].astype(f32), axis=0).astype(bf16)
    for hot_ref, out_ref in ((hot_there_ref, there_ref), (hot_here_ref, here_ref)):
        got = jnp.dot(hot_ref[...], own, preferred_element_type=f32)
        out_ref[...] = got.astype(bf16)


def back_rows(hot_here, hot_there, parts):
    half, n_own = hot_here.shape
    part = parts.shape[2]
    return call(
        back_body,
        (jax.ShapeDtypeStruct((half, part), bf16),) * 2,
        (4 * half * n_own * part, 4 * half * part + 2 * parts.size),
    )(hot_here, hot_there, parts)


def unpack_body(parts_ref, out_ref):
    n_tok = out_ref.shape[0]
    added = jnp.sum(parts_ref[...].astype(f32), axis=0)
    pieces = [added[i * n_tok : (i + 1) * n_tok] for i in range(SPLIT)]
    out_ref[...] = jnp.concatenate(pieces, axis=1).astype(bf16)


def unpack(parts, n_tok):
    return call(
        unpack_body,
        jax.ShapeDtypeStruct((n_tok, SPLIT * parts.shape[2]), bf16),
        (parts.size, 2 * parts.size),
    )(parts)


def local(out_grad, expert_ids, slot_ids, gate_q, saved_x, w_gate, w_up, w_down):
    n_grp, n_node = lax.axis_size("grp"), lax.axis_size("node")
    my_expert, my_node = lax.axis_index("grp"), lax.axis_index("node")
    n_rest, n_z = n_node // SPLIT, n_grp // C_DEV
    block = [[h * SPLIT + d for d in range(SPLIT)] for h in range(n_rest)]
    along_z = [
        [z * C_DEV + (c + z // 2) % C_DEV for z in range(n_z)] for c in range(C_DEV)
    ]
    other = [(z * C_DEV + c, z * C_DEV + 1 - c) for z in range(n_z) for c in range(C_DEV)]
    n_tok, width = out_grad.shape
    part = width // SPLIT
    n_slot = saved_x.shape[1]
    per_node = n_slot // n_node
    n_hid = w_down.shape[1]
    n_pick = expert_ids.shape[1]
    n_own = SPLIT * per_node
    gate, up, down = w_gate[0].T, w_up[0].T, w_down[0]

    payload = pack(my_node.astype(jnp.int32).reshape(1), out_grad, expert_ids, slot_ids, gate_q, per_node)

    weights = cut_weights(gate, up, down)
    payload, weights = lax.optimization_barrier((payload, weights))
    weights = swap(weights, "node", block)

    here = lax.all_gather(payload, "grp", axis=0, axis_index_groups=along_z, tiled=True)
    there = lax.ppermute(here, "grp", other)
    expert = my_expert.astype(jnp.int32).reshape(1)
    rows, hot_here = select(expert, here, (), 1, n_tok, per_node, n_pick)
    rows, hot_there = select(expert, there, (rows,), n_rest, n_tok, per_node, n_pick)
    late = (my_expert % C_DEV).astype(jnp.int32).reshape(1)
    gate, rows = lax.optimization_barrier((gate, rows))
    coef = early_forward(late, saved_x[0], gate, up)
    rows, weights, coef = lax.optimization_barrier((rows, weights, coef))
    rows = lax.all_to_all(rows, "node", 0, 0, tiled=True)

    gate, rows = lax.optimization_barrier((gate, rows))
    hidden = swap(hidden_part(weights, rows), "node", block)
    hidden = hidden.reshape(SPLIT, n_hid, n_slot)
    coef = late_forward(1 - late, saved_x[0], gate, up, coef)
    grads = swap(grads_of(hidden, coef), "node", block)
    parts = lax.all_to_all(slot_part(grads, weights), "node", 0, 0, tiled=True)

    here, there = back_rows(hot_here, hot_there, parts.reshape(n_rest, n_own, part))
    back = total([here, lax.ppermute(there, "grp", other)])
    back = swap(back, "grp", along_z).reshape(n_z, SPLIT * n_tok, part)
    return unpack(back, n_tok)


def solution(mesh):
    in_specs = (
        P(("grp", "node"), None),
        P(("grp", "node"), None),
        P(("grp", "node"), None),
        P(("grp", "node"), None),
        P("grp", None, None),
        P("grp", None, "node"),
        P("grp", None, "node"),
        P("grp", "node", None),
    )
    out_specs = P(("grp", "node"), None)
    return jax.shard_map(local, mesh=mesh, in_specs=in_specs, out_specs=out_specs, check_vma=False)
```
